256 devices in a mesh: tensor: 2 (over z_hi), fsdp: 32 (over x, z_lo, core), island: 4 (over y).
Axes of the slice: x: 4, y: 4, z: 8 (z_hi: 2, z_lo: 4; z = z_hi * 4 + z_lo), core: 2. Of those that a mesh axis runs over, the one named last changes fastest.
Arguments:
- activations: bfloat16 [4, 16384, 1024], P('island', 'fsdp', 'tensor'), may hold values from -6 to 6
- out_grads: bfloat16 [4, 16384, 2048], P('island', 'fsdp', 'tensor'), may hold values from -6 to 6
- moment: float32 [4, 2, 1024, 1024], P('island', 'tensor', 'fsdp'), may hold values from -6 to 6
- moment_sq: float32 [4, 2, 1024, 1024], P('island', 'tensor', 'fsdp'), may hold values from 0.05 to 2
- left_factor: float32 [4, 2, 1024, 1024], P('island', 'tensor', 'fsdp'), may hold values from -1 to 7, as said below
- right_factor: float32 [4, 2, 1024, 1024], P('island', 'tensor', 'fsdp'), may hold values from -1 to 7, as said below
- left_basis: bfloat16 [4, 2, 1024, 1024], P('island', 'tensor'), may hold values from -1 to 2
- right_basis: bfloat16 [4, 2, 1024, 1024], P('island', 'tensor'), may hold values from -1 to 2
- params: float32 [4, 2, 1024, 1024], P('island', 'tensor', 'fsdp'), may hold values from -6 to 6
- anchor: float32 [2, 1024, 1024], P('tensor', 'fsdp'), may hold values from -6 to 6
- outer_momentum: float32 [2, 1024, 1024], P('tensor', 'fsdp'), may hold values from -3 to 3
Outputs:
- anchor_new: float32 [2, 1024, 1024], P('tensor', 'fsdp')
- momentum_new: float32 [2, 1024, 1024], P('tensor', 'fsdp')
- moment_new: float32 [4, 2, 1024, 1024], P('island', 'tensor', 'fsdp')
- moment_sq_new: float32 [4, 2, 1024, 1024], P('island', 'tensor', 'fsdp')
- left_factor_new: float32 [4, 2, 1024, 1024], P('island', 'tensor', 'fsdp')
- right_factor_new: float32 [4, 2, 1024, 1024], P('island', 'tensor', 'fsdp')
- left_basis_new: bfloat16 [4, 2, 1024, 1024], P('island', 'tensor')
- right_basis_new: bfloat16 [4, 2, 1024, 1024], P('island', 'tensor')
The draws below stay inside these ranges and needn't reach their ends.
Inputs may be any that keep to these rules, and one draw needn't show every extreme that they name: `left_factor`: each matrix is symmetric, and each diagonal entry exceeds the sum of magnitudes of the other entries of its row. `right_factor`: each matrix is symmetric, and each diagonal entry exceeds the sum of magnitudes of the other entries of its row.
All inputs are finite; a program needn't handle non-finite values.
Results may differ from the reference program's by a relative error of at most 0.0059.
Values may be sent and summed in bfloat16 or wider, within the bound.
A program may use at most 128 MiB of HBM per device.

```python
import math
import jax
import jax.numpy as jnp
from jax import lax

BLOCK = 1024
TOKENS = 16384
REPLICAS = 4
BANDS = 2


def dominant(entries, diag_lift):
    coupled = (entries + jnp.swapaxes(entries, -1, -2)) * (1.5 / BLOCK)
    identity = jnp.eye(BLOCK, dtype=jnp.float32)
    return coupled * (1.0 - identity) + (3.0 + diag_lift)[..., None] * identity


def near_basis(entries):
    identity = jnp.eye(BLOCK, dtype=jnp.float32)
    return (identity + entries * (0.5 / math.sqrt(BLOCK))).astype(jnp.bfloat16)


def draw_left_factor(key, part):
    key = jax.random.fold_in(key, 11)
    noise_key, lift_key = jax.random.split(key)
    full_shape = (REPLICAS, BANDS, BLOCK, BLOCK)
    entries = jax.random.uniform(noise_key, full_shape, jnp.float32, -1.0, 1.0)
    diag_lift = jax.random.uniform(lift_key, (REPLICAS, BANDS, BLOCK), jnp.float32, 0.5, 3.0)
    return dominant(entries, diag_lift)


def draw_right_factor(key, part):
    key = jax.random.fold_in(key, 17)
    noise_key, lift_key = jax.random.split(key)
    full_shape = (REPLICAS, BANDS, BLOCK, BLOCK)
    entries = jax.random.uniform(noise_key, full_shape, jnp.float32, -1.0, 1.0)
    diag_lift = jax.random.uniform(lift_key, (REPLICAS, BANDS, BLOCK), jnp.float32, 0.5, 3.0)
    return dominant(entries, diag_lift)


def draw_left_basis(key, part):
    key = jax.random.fold_in(key, 23)
    full_shape = (REPLICAS, BANDS, BLOCK, BLOCK)
    entries = jnp.clip(jax.random.normal(key, full_shape, jnp.float32), -4.0, 4.0)
    return near_basis(entries)


def draw_right_basis(key, part):
    key = jax.random.fold_in(key, 29)
    full_shape = (REPLICAS, BANDS, BLOCK, BLOCK)
    entries = jnp.clip(jax.random.normal(key, full_shape, jnp.float32), -4.0, 4.0)
    return near_basis(entries)


def levels(rng, dims, cuts, low, largest):
    loudness = 1.0
    for axis_at, blocks in cuts:
        heights = jax.random.uniform(jax.random.fold_in(jax.random.fold_in(rng, 6), axis_at), (blocks,), jnp.float32, low / len(cuts), largest / len(cuts))
        loudness = loudness * jnp.repeat(jnp.exp(heights), dims[axis_at] // blocks).reshape((-1,) + (1,) * (len(dims) - 1 - axis_at))
    return loudness


def noise(stream_key, extent, scale, limit, cuts=(), kind=jnp.bfloat16):
    array = scale * jax.random.normal(stream_key, extent, jnp.float32)
    if cuts:
        array = array * levels(stream_key, extent, cuts, -0.22, 0.18)
    return jnp.clip(array, -limit, limit).astype(kind)


def setup_inputs(seed: int = 0) -> dict:
    streams_of = jax.random.split(jax.random.key(seed), 12)
    return {
        "activations": noise(streams_of[0], (REPLICAS, TOKENS, BLOCK), 1.0, 6.0, ((0, 4), (1, 32), (2, 2))),
        "out_grads": noise(streams_of[1], (REPLICAS, TOKENS, BANDS * BLOCK), 1.0, 6.0, ((0, 4), (1, 32), (2, 2))),
        "moment": noise(streams_of[2], (REPLICAS, BANDS, BLOCK, BLOCK), 1.0, 6.0, ((0, 4), (1, 2), (2, 32)), jnp.float32),
        "moment_sq": jnp.clip(jnp.exp(math.log(2.0) - 3.6888794 * jax.random.uniform(streams_of[3], (REPLICAS, BANDS, BLOCK, BLOCK), jnp.float32) ** levels(streams_of[3], (REPLICAS, BANDS, BLOCK, BLOCK), ((0, 4), (1, 2), (2, 32)), -0.2, 0.2)), 0.05, 2.0),
        "left_factor": draw_left_factor(jax.random.fold_in(streams_of[11], 71), 0),
        "right_factor": draw_right_factor(jax.random.fold_in(streams_of[11], 71), 0),
        "left_basis": draw_left_basis(jax.random.fold_in(streams_of[11], 71), 0),
        "right_basis": draw_right_basis(jax.random.fold_in(streams_of[11], 71), 0),
        "params": noise(streams_of[8], (REPLICAS, BANDS, BLOCK, BLOCK), 1.0, 6.0, ((0, 4), (1, 2), (2, 32)), jnp.float32),
        "anchor": noise(streams_of[9], (BANDS, BLOCK, BLOCK), 1.0, 6.0, ((0, 2), (1, 32)), jnp.float32),
        "outer_momentum": noise(streams_of[10], (BANDS, BLOCK, BLOCK), 0.5, 3.0, ((0, 2), (1, 32)), jnp.float32),
    }


BETA_ONE = 0.9
BETA_TWO = 0.95
FACTOR_BETA = 0.9
ADAM_EPS = 1e-08
INNER_RATE = 0.5
OUTER_RATE = 0.7
OUTER_MOMENT = 0.9

def mixed_dot(left, right):
    return jnp.dot(left.astype(jnp.float32), right.astype(jnp.float32), preferred_element_type=jnp.float32)

def exact_dot(left, right):
    return jnp.dot(left.astype(jnp.float32), right.astype(jnp.float32), precision=lax.Precision.HIGHEST, preferred_element_type=jnp.float32)

def refresh(factor, basis):
    power = mixed_dot(factor.astype(jnp.bfloat16), basis).astype(jnp.bfloat16)
    gram = mixed_dot(power.T, power)
    lower = jnp.linalg.cholesky(gram)
    solved = jax.scipy.linalg.solve_triangular(lower, power.T.astype(jnp.float32), lower=True)
    return solved.T.astype(jnp.bfloat16)

def reference(activations, out_grads, moment, moment_sq, left_factor, right_factor, left_basis, right_basis, params, anchor, outer_momentum):
    grad_scale = 1.0 / math.sqrt(TOKENS)
    moments, squares, lefts, rights, left_bases, right_bases = ([], [], [], [], [], [])
    delta_sum = jnp.zeros((BANDS, BLOCK, BLOCK), jnp.float32)
    for island in range(REPLICAS):
        band_grads = mixed_dot(activations[island].T, out_grads[island]) * grad_scale
        row_m, row_s, row_l, row_r, row_lb, row_rb, row_d = ([], [], [], [], [], [], [])
        for band in range(BANDS):
            gradient = band_grads[:, band * BLOCK:(band + 1) * BLOCK].astype(jnp.bfloat16)
            left_old = left_basis[island, band]
            right_old = right_basis[island, band]
            half_turn = mixed_dot(left_old.T, gradient).astype(jnp.bfloat16)
            rotated = mixed_dot(half_turn, right_old)
            first_moment = BETA_ONE * moment[island, band] + (1.0 - BETA_ONE) * rotated
            second_moment = BETA_TWO * moment_sq[island, band] + (1.0 - BETA_TWO) * rotated * rotated
            normed = (first_moment / (jnp.sqrt(second_moment) + ADAM_EPS)).astype(jnp.bfloat16)
            back_half = mixed_dot(left_old, normed).astype(jnp.bfloat16)
            update = mixed_dot(back_half, right_old.T)
            left_next = FACTOR_BETA * left_factor[island, band] + (1.0 - FACTOR_BETA) * mixed_dot(gradient, gradient.T) / BLOCK
            right_next = FACTOR_BETA * right_factor[island, band] + (1.0 - FACTOR_BETA) * mixed_dot(gradient.T, gradient) / BLOCK
            left_new = refresh(left_next, left_old)
            right_new = refresh(right_next, right_old)
            turn_left = mixed_dot(left_new.T, left_old)
            turn_right = mixed_dot(right_old.T, right_new)
            carried = exact_dot(turn_left, exact_dot(first_moment, turn_right))
            row_d.append(anchor[band] - (params[island, band] - INNER_RATE * update))
            row_m.append(carried)
            row_s.append(second_moment)
            row_l.append(left_next)
            row_r.append(right_next)
            row_lb.append(left_new)
            row_rb.append(right_new)
        delta_sum = delta_sum + jnp.stack(row_d)
        moments.append(jnp.stack(row_m))
        squares.append(jnp.stack(row_s))
        lefts.append(jnp.stack(row_l))
        rights.append(jnp.stack(row_r))
        left_bases.append(jnp.stack(row_lb))
        right_bases.append(jnp.stack(row_rb))
    average = delta_sum / REPLICAS
    momentum_new = OUTER_MOMENT * outer_momentum + average
    anchor_new = anchor - OUTER_RATE * (average + OUTER_MOMENT * momentum_new)
    return (anchor_new, momentum_new, jnp.stack(moments), jnp.stack(squares), jnp.stack(lefts), jnp.stack(rights), jnp.stack(left_bases), jnp.stack(right_bases))
```

```python
import math

import jax
import jax.numpy as jnp
from jax import lax
from jax.experimental import pallas as pl
from jax.experimental.pallas import tpu as pltpu
from jax.sharding import PartitionSpec as P

BETA_ONE = 0.9
BETA_TWO = 0.95
FACTOR_BETA = 0.9
ADAM_EPS = 1e-08
INNER_RATE = 0.5
OUTER_RATE = 0.7
OUTER_MOMENT = 0.9
RESIDUAL_LIMIT = 0.06

N = 1024
H = 512
Q4 = 256
ROUGH = 4


def nn(a, b):
    return jnp.dot(a, b, preferred_element_type=jnp.float32)


def nt(a, b):
    return lax.dot_general(a, b, (((1,), (1,)), ((), ())), preferred_element_type=jnp.float32)


def split(x):
    hi = x.astype(jnp.bfloat16)
    return hi, (x - hi.astype(jnp.float32)).astype(jnp.bfloat16)


def nt3(a, b):
    return nt(a[0], b[0]) + (nt(a[0], b[1]) + nt(a[1], b[0]))


def nn3(a, b):
    return nn(a[0], b[0]) + (nn(a[0], b[1]) + nn(a[1], b[0]))


def iotas(n):
    return lax.broadcasted_iota(jnp.int32, (n, n), 0), lax.broadcasted_iota(jnp.int32, (n, n), 1)


def low(e):
    r, c = iotas(e.shape[0])
    return jnp.where(r > c, e, jnp.where(r == c, 0.5 * e, 0.0))


def minus_eye(e):
    r, c = iotas(e.shape[0])
    return jnp.where(r == c, e - 1.0, e)


def diag_rows(s):
    r, c = iotas(s.shape[0])
    picked = jnp.where(r == c, s, 0.0)
    return jnp.sum(picked, 1, keepdims=True), jnp.sum(picked, 0, keepdims=True)


def residual(x, s, y_ref):
    a, b = slice(0, Q4), slice(Q4, H)
    if len(x) == 1:
        xa, x2 = x[0][a, a], x[0][b, :]
        ya = nn(xa, s[0][a, a]).astype(jnp.bfloat16)
        y2 = nn(x2, s[0][...]).astype(jnp.bfloat16)
        return nt(ya, xa), nt(y2[:, a], xa), nt(y2, x2)
    xa = (x[0][a, a], x[1][a, a])
    x2 = (x[0][b, :], x[1][b, :])
    ya = split(nn3(xa, (s[0][a, a], s[1][a, a])))
    y2 = split(nn3(x2, (s[0][...], s[1][...])))
    y2a = (y2[0][:, a], y2[1][:, a])
    return nt3(ya, xa), nt3(y2a, xa), nt3(y2, x2)


def leaf(s_ref, x_ref, sh, sl, xh, xl):
    a, b = slice(0, Q4), slice(Q4, H)
    dc, dr = diag_rows(s_ref[...])
    dc, dr = lax.rsqrt(dc), lax.rsqrt(dr)
    sn = s_ref[...] * dc * dr
    hi, lo = split(sn)
    sh[...] = hi
    sl[...] = lo
    e0 = minus_eye(sn)
    f0 = low(e0)
    r, c = iotas(H)
    x0 = jnp.where(r == c, 1.0 - f0, -f0)
    x_ref[...] = x0
    xh[...] = x0.astype(jnp.bfloat16)

    def update(e, fine):
        eaa, eca, edd = e
        faa, fdd = low(eaa).astype(jnp.bfloat16), low(edd).astype(jnp.bfloat16)
        fca = eca.astype(jnp.bfloat16)
        xa, xc, xd = xh[a, a], xh[b, a], xh[b, b]
        na = x_ref[a, a] - nn(faa, xa)
        nc = x_ref[b, a] - (nn(fca, xa) + nn(fdd, xc))
        nd = x_ref[b, b] - nn(fdd, xd)
        x_ref[a, a] = na
        x_ref[b, a] = nc
        x_ref[b, b] = nd
        if not fine:
            xh[a, a] = na.astype(jnp.bfloat16)
            xh[b, a] = nc.astype(jnp.bfloat16)
            xh[b, b] = nd.astype(jnp.bfloat16)

    def step(_, carry):
        eaa, eca, edd = residual((xh,), (sh,), None)
        update((minus_eye(eaa), eca, minus_eye(edd)), False)
        return carry

    lax.fori_loop(0, ROUGH, step, 0)
    hi, lo = split(x_ref[...])
    xh[...] = hi
    xl[...] = lo
    eaa, eca, edd = residual((xh, xl), (sh, sl), None)
    eaa, edd = minus_eye(eaa), minus_eye(edd)
    left = jnp.sum(eaa * eaa) + 2.0 * jnp.sum(eca * eca) + jnp.sum(edd * edd)
    update((eaa, eca, edd), True)
    x_ref[...] = x_ref[...] * dr
    hi, lo = split(x_ref[...])
    xh[...] = hi
    xl[...] = lo
    return left


def orth_body(p_ref, q_ref, res_ref, pt, s_ref, a21, x_ref, sh, sl, xh, xl, l21h, l21l):
    f, g = slice(0, H), slice(H, N)
    a, b = slice(0, Q4), slice(Q4, H)
    pt[...] = p_ref[...].T
    s_ref[...] = nt(pt[f, :], pt[f, :])
    a21[...] = nt(pt[g, :], pt[f, :])
    r1 = leaf(s_ref, x_ref, sh, sl, xh, xl)

    def by_x(t):
        ta = tuple(v[:, a] for v in t)
        xa, x2 = (xh[a, a], xl[a, a]), (xh[b, :], xl[b, :])
        if len(t) == 1:
            return nt(ta[0], xa[0]) + nt(ta[0], xa[1]), nt(t[0], x2[0]) + nt(t[0], x2[1])
        return nt3(ta, xa), nt3(t, x2)

    def l_rows(i, c):
        rows = pl.ds(pl.multiple_of(i * Q4, Q4), Q4)
        u, v = by_x(split(a21[rows, :]))
        uh, ul = split(u)
        vh, vl = split(v)
        l21h[rows, a] = uh
        l21h[rows, b] = vh
        l21l[rows, a] = ul
        l21l[rows, b] = vl
        return c
    lax.fori_loop(0, 2, l_rows, 0)

    def q1_rows(i, c):
        rows = pl.ds(pl.multiple_of(i * Q4, Q4), Q4)
        u, v = by_x((p_ref[rows, f],))
        uh, ul = split(u)
        vh, vl = split(v)
        q_ref[rows, a] = uh
        q_ref[rows, Q4:H] = vh
        pt[rows, a] = ul
        pt[rows, Q4:H] = vl
        return c

    s_ref[...] = nt(pt[g, :], pt[g, :]) - nt3((l21h[...], l21l[...]), (l21h[...], l21l[...]))
    lax.fori_loop(0, 4, q1_rows, 0)
    r2 = leaf(s_ref, x_ref, sh, sl, xh, xl)

    def q2_rows(i, c):
        rows = pl.ds(pl.multiple_of(i * Q4, Q4), Q4)
        t = p_ref[rows, g].astype(jnp.float32) - nt3((q_ref[rows, f], pt[rows, f]), (l21h[...], l21l[...]))
        u, v = by_x(split(t))
        q_ref[rows, H:H + Q4] = u.astype(jnp.bfloat16)
        q_ref[rows, H + Q4:N] = v.astype(jnp.bfloat16)
        return c
    lax.fori_loop(0, 4, q2_rows, 0)
    res_ref[...] = jnp.full((8, 128), jnp.maximum(r1, r2), jnp.float32)


def orth(p):
    bf, f32 = jnp.bfloat16, jnp.float32
    return pl.pallas_call(
        orth_body,
        out_shape=(jax.ShapeDtypeStruct((N, N), bf), jax.ShapeDtypeStruct((8, 128), f32)),
        in_specs=[pl.BlockSpec(memory_space=pltpu.VMEM)],
        out_specs=(pl.BlockSpec(memory_space=pltpu.VMEM),) * 2,
        scratch_shapes=[
            pltpu.VMEM((N, N), bf), pltpu.VMEM((H, H), f32), pltpu.VMEM((H, H), f32), pltpu.VMEM((H, H), f32),
        ] + [pltpu.VMEM((H, H), bf)] * 6,
        compiler_params=pltpu.CompilerParams(vmem_limit_bytes=40 * 1024 * 1024),
    )(p)


def mixed_dot(left, right):
    return jnp.dot(left, right, preferred_element_type=jnp.float32)


def two_pass(wide, narrow):
    rows = wide.shape[0]
    both = mixed_dot(jnp.concatenate(split(wide), 0), narrow)
    return both[:rows] + both[rows:]


def blocked_cholesky(grams):
    order = grams.shape[-1]
    half = order // 2
    upper_left = grams[:, :half, :half]
    lower_left = grams[:, half:, :half]
    lower_right = grams[:, half:, half:]
    head = jnp.linalg.cholesky(upper_left)
    panel_t = jax.scipy.linalg.solve_triangular(head, jnp.swapaxes(lower_left, 1, 2), lower=True)
    panel = jnp.swapaxes(panel_t, 1, 2)
    schur = lower_right - jnp.einsum("bik,bjk->bij", panel, panel, precision=lax.Precision.HIGHEST)
    tail = jnp.linalg.cholesky(schur)
    zeros_block = jnp.zeros_like(lower_left)
    top = jnp.concatenate([head, jnp.swapaxes(zeros_block, 1, 2)], axis=2)
    bottom = jnp.concatenate([panel, tail], axis=2)
    return jnp.concatenate([top, bottom], axis=1)


def exact_orth(power):
    lower = blocked_cholesky(mixed_dot(power.T, power)[None])[0]
    solved = jax.scipy.linalg.solve_triangular(lower, power.T.astype(jnp.float32), lower=True)
    return solved.T.astype(jnp.bfloat16)


def orthonormal(power):
    quick, residual = orth(power)
    return lax.cond(residual[0, 0] < RESIDUAL_LIMIT, lambda: quick, lambda: exact_orth(power))


def per_device(
    activations,
    out_grads,
    moment,
    moment_sq,
    left_factor,
    right_factor,
    left_basis,
    right_basis,
    params,
    anchor,
    outer_momentum,
):
    features = lax.all_gather(activations[0], "tensor", axis=1, tiled=True)
    grad_rows = out_grads[0]
    owners = lax.axis_size("fsdp")
    row_count = left_factor.shape[2]
    block_width = features.shape[1]
    grad_scale = 1.0 / math.sqrt(features.shape[0] * owners)
    core = lax.axis_index("fsdp") % 2
    first_row = lax.axis_index("fsdp") * row_count
    own_rows = lax.psum_scatter(
        mixed_dot(features.T, grad_rows) * grad_scale, "fsdp", scatter_dimension=0, tiled=True
    ).astype(jnp.bfloat16)
    gradient_full = lax.all_gather(own_rows, "fsdp", axis=0, tiled=True)
    left_old = left_basis[0, 0]
    right_old = right_basis[0, 0]
    left_columns = lax.dynamic_slice_in_dim(left_old, first_row, row_count, 1)
    half_turn = mixed_dot(left_columns.T, gradient_full).astype(jnp.bfloat16)
    rotated = mixed_dot(half_turn, right_old)
    first_moment = BETA_ONE * moment[0, 0] + (1.0 - BETA_ONE) * rotated
    second_moment = BETA_TWO * moment_sq[0, 0] + (1.0 - BETA_TWO) * rotated * rotated
    normed = (first_moment / (jnp.sqrt(second_moment) + ADAM_EPS)).astype(jnp.bfloat16)
    own_columns = lax.dynamic_slice_in_dim(gradient_full, first_row, row_count, 1)
    left_next = (
        FACTOR_BETA * left_factor[0, 0]
        + (1.0 - FACTOR_BETA) * mixed_dot(own_rows, gradient_full.T) / block_width
    )
    right_next = (
        FACTOR_BETA * right_factor[0, 0]
        + (1.0 - FACTOR_BETA) * mixed_dot(own_columns.T, gradient_full) / block_width
    )
    power_left = mixed_dot(left_next.astype(jnp.bfloat16), left_old).astype(jnp.bfloat16)
    power_right = mixed_dot(right_next.astype(jnp.bfloat16), right_old).astype(jnp.bfloat16)
    power_left_all = lax.all_gather(power_left, "fsdp", axis=0, tiled=True)
    power_right_all = lax.all_gather(power_right, "fsdp", axis=0, tiled=True)
    normed_all = lax.all_gather(normed, "fsdp", axis=0, tiled=True)
    first_all = lax.all_gather(first_moment, "fsdp", axis=0, tiled=True)
    mine = orthonormal(jnp.where(core == 0, power_left_all, power_right_all))
    other = lax.ppermute(mine, "fsdp", [(d, d ^ 1) for d in range(owners)])
    left_new = jnp.where(core == 0, mine, other)
    right_new = jnp.where(core == 0, other, mine)
    left_rows = lax.dynamic_slice_in_dim(left_old, first_row, row_count, 0)
    back_half = mixed_dot(left_rows, normed_all).astype(jnp.bfloat16)
    update = mixed_dot(back_half, right_old.T)
    new_columns = lax.dynamic_slice_in_dim(left_new, first_row, row_count, 1)
    turn_rows = mixed_dot(new_columns.T, left_old)
    high_first, low_first = split(first_all)
    moment_next = two_pass(turn_rows, high_first) + mixed_dot(turn_rows.astype(jnp.bfloat16), low_first)
    moment_next = two_pass(two_pass(moment_next, right_old.T), right_new)
    island_delta = anchor[0] - (params[0, 0] - INNER_RATE * update)
    average = lax.psum(island_delta, "island") / lax.axis_size("island")
    momentum_next = OUTER_MOMENT * outer_momentum[0] + average
    anchor_next = anchor[0] - OUTER_RATE * (average + OUTER_MOMENT * momentum_next)
    return (
        anchor_next[None],
        momentum_next[None],
        moment_next[None, None],
        second_moment[None, None],
        left_next[None, None],
        right_next[None, None],
        left_new[None, None],
        right_new[None, None],
    )


def solution(mesh):
    in_specs = (
        P("island", "fsdp", "tensor"),
        P("island", "fsdp", "tensor"),
        P("island", "tensor", "fsdp", None),
        P("island", "tensor", "fsdp", None),
        P("island", "tensor", "fsdp", None),
        P("island", "tensor", "fsdp", None),
        P("island", "tensor", None, None),
        P("island", "tensor", None, None),
        P("island", "tensor", "fsdp", None),
        P("tensor", "fsdp", None),
        P("tensor", "fsdp", None),
    )
    out_specs = (
        P("tensor", "fsdp", None),
        P("tensor", "fsdp", None),
        P("island", "tensor", "fsdp", None),
        P("island", "tensor", "fsdp", None),
        P("island", "tensor", "fsdp", None),
        P("island", "tensor", "fsdp", None),
        P("island", "tensor", None, None),
        P("island", "tensor", None, None),
    )
    return jax.shard_map(
        per_device, mesh=mesh, in_specs=in_specs, out_specs=out_specs, check_vma=False
    )
```

```python
import functools
import math

import jax
import jax.numpy as jnp
from jax import lax
from jax.experimental import pallas as pl
from jax.experimental.pallas import tpu as pltpu
from jax.sharding import PartitionSpec as P

BETA_ONE = 0.9
BETA_TWO = 0.95
FACTOR_BETA = 0.9
ADAM_EPS = 1e-08
INNER_RATE = 0.5
OUTER_RATE = 0.7
OUTER_MOMENT = 0.9
RESIDUAL_LIMIT = 0.06

N = 1024
H = 512
Q4 = 256
ROUGH = 4


def nn(a, b):
    return jnp.dot(a, b, preferred_element_type=jnp.float32)


def nt(a, b):
    return lax.dot_general(a, b, (((1,), (1,)), ((), ())), preferred_element_type=jnp.float32)


def split(x):
    hi = x.astype(jnp.bfloat16)
    return hi, (x - hi.astype(jnp.float32)).astype(jnp.bfloat16)


def nt3(a, b):
    return nt(a[0], b[0]) + (nt(a[0], b[1]) + nt(a[1], b[0]))


def nn3(a, b):
    return nn(a[0], b[0]) + (nn(a[0], b[1]) + nn(a[1], b[0]))


def iotas(n):
    return lax.broadcasted_iota(jnp.int32, (n, n), 0), lax.broadcasted_iota(jnp.int32, (n, n), 1)


def low(e):
    r, c = iotas(e.shape[0])
    return jnp.where(r > c, e, jnp.where(r == c, 0.5 * e, 0.0))


def minus_eye(e):
    r, c = iotas(e.shape[0])
    return jnp.where(r == c, e - 1.0, e)


def diag_rows(s):
    r, c = iotas(s.shape[0])
    picked = jnp.where(r == c, s, 0.0)
    return jnp.sum(picked, 1, keepdims=True), jnp.sum(picked, 0, keepdims=True)


def residual(x, s, y_ref):
    a, b = slice(0, Q4), slice(Q4, H)
    if len(x) == 1:
        xa, x2 = x[0][a, a], x[0][b, :]
        ya = nn(xa, s[0][a, a]).astype(jnp.bfloat16)
        y2 = nn(x2, s[0][...]).astype(jnp.bfloat16)
        return nt(ya, xa), nt(y2[:, a], xa), nt(y2, x2)
    xa = (x[0][a, a], x[1][a, a])
    x2 = (x[0][b, :], x[1][b, :])
    ya = split(nn3(xa, (s[0][a, a], s[1][a, a])))
    y2 = split(nn3(x2, (s[0][...], s[1][...])))
    y2a = (y2[0][:, a], y2[1][:, a])
    return nt3(ya, xa), nt3(y2a, xa), nt3(y2, x2)


def leaf(s_ref, x_ref, sh, sl, xh, xl):
    a, b = slice(0, Q4), slice(Q4, H)
    dc, dr = diag_rows(s_ref[...])
    dc, dr = lax.rsqrt(dc), lax.rsqrt(dr)
    sn = s_ref[...] * dc * dr
    hi, lo = split(sn)
    sh[...] = hi
    sl[...] = lo
    e0 = minus_eye(sn)
    f0 = low(e0)
    r, c = iotas(H)
    x0 = jnp.where(r == c, 1.0 - f0, -f0)
    x_ref[...] = x0
    xh[...] = x0.astype(jnp.bfloat16)

    def update(e, fine):
        eaa, eca, edd = e
        faa, fdd = low(eaa).astype(jnp.bfloat16), low(edd).astype(jnp.bfloat16)
        fca = eca.astype(jnp.bfloat16)
        xa, xc, xd = xh[a, a], xh[b, a], xh[b, b]
        na = x_ref[a, a] - nn(faa, xa)
        nc = x_ref[b, a] - (nn(fca, xa) + nn(fdd, xc))
        nd = x_ref[b, b] - nn(fdd, xd)
        x_ref[a, a] = na
        x_ref[b, a] = nc
        x_ref[b, b] = nd
        if not fine:
            xh[a, a] = na.astype(jnp.bfloat16)
            xh[b, a] = nc.astype(jnp.bfloat16)
            xh[b, b] = nd.astype(jnp.bfloat16)

    def step(_, carry):
        eaa, eca, edd = residual((xh,), (sh,), None)
        update((minus_eye(eaa), eca, minus_eye(edd)), False)
        return carry

    lax.fori_loop(0, ROUGH, step, 0)
    hi, lo = split(x_ref[...])
    xh[...] = hi
    xl[...] = lo
    eaa, eca, edd = residual((xh, xl), (sh, sl), None)
    eaa, edd = minus_eye(eaa), minus_eye(edd)
    left = jnp.sum(eaa * eaa) + 2.0 * jnp.sum(eca * eca) + jnp.sum(edd * edd)
    update((eaa, eca, edd), True)
    x_ref[...] = x_ref[...] * dr
    hi, lo = split(x_ref[...])
    xh[...] = hi
    xl[...] = lo
    return left


def orth_body(p_ref, q_ref, res_ref, pt, s_ref, a21, x_ref, sh, sl, xh, xl, l21h, l21l):
    f, g = slice(0, H), slice(H, N)
    a, b = slice(0, Q4), slice(Q4, H)
    pt[...] = p_ref[...].T
    s_ref[...] = nt(pt[f, :], pt[f, :])
    a21[...] = nt(pt[g, :], pt[f, :])
    r1 = leaf(s_ref, x_ref, sh, sl, xh, xl)

    def by_x(t):
        ta = tuple(v[:, a] for v in t)
        xa, x2 = (xh[a, a], xl[a, a]), (xh[b, :], xl[b, :])
        if len(t) == 1:
            return nt(ta[0], xa[0]) + nt(ta[0], xa[1]), nt(t[0], x2[0]) + nt(t[0], x2[1])
        return nt3(ta, xa), nt3(t, x2)

    def l_rows(i, c):
        rows = pl.ds(pl.multiple_of(i * Q4, Q4), Q4)
        u, v = by_x(split(a21[rows, :]))
        uh, ul = split(u)
        vh, vl = split(v)
        l21h[rows, a] = uh
        l21h[rows, b] = vh
        l21l[rows, a] = ul
        l21l[rows, b] = vl
        return c
    lax.fori_loop(0, 2, l_rows, 0)

    def q1_rows(i, c):
        rows = pl.ds(pl.multiple_of(i * Q4, Q4), Q4)
        u, v = by_x((p_ref[rows, f],))
        uh, ul = split(u)
        vh, vl = split(v)
        q_ref[rows, a] = uh
        q_ref[rows, Q4:H] = vh
        pt[rows, a] = ul
        pt[rows, Q4:H] = vl
        return c

    s_ref[...] = nt(pt[g, :], pt[g, :]) - nt3((l21h[...], l21l[...]), (l21h[...], l21l[...]))
    lax.fori_loop(0, 4, q1_rows, 0)
    r2 = leaf(s_ref, x_ref, sh, sl, xh, xl)

    def q2_rows(i, c):
        rows = pl.ds(pl.multiple_of(i * Q4, Q4), Q4)
        t = p_ref[rows, g].astype(jnp.float32) - nt3((q_ref[rows, f], pt[rows, f]), (l21h[...], l21l[...]))
        u, v = by_x(split(t))
        q_ref[rows, H:H + Q4] = u.astype(jnp.bfloat16)
        q_ref[rows, H + Q4:N] = v.astype(jnp.bfloat16)
        return c
    lax.fori_loop(0, 4, q2_rows, 0)
    res_ref[...] = jnp.full((8, 128), jnp.maximum(r1, r2), jnp.float32)


def orth(p):
    bf, f32 = jnp.bfloat16, jnp.float32
    return pl.pallas_call(
        orth_body,
        out_shape=(jax.ShapeDtypeStruct((N, N), bf), jax.ShapeDtypeStruct((8, 128), f32)),
        in_specs=[pl.BlockSpec(memory_space=pltpu.VMEM)],
        out_specs=(pl.BlockSpec(memory_space=pltpu.VMEM),) * 2,
        scratch_shapes=[
            pltpu.VMEM((N, N), bf), pltpu.VMEM((H, H), f32), pltpu.VMEM((H, H), f32), pltpu.VMEM((H, H), f32),
        ] + [pltpu.VMEM((H, H), bf)] * 6,
        compiler_params=pltpu.CompilerParams(vmem_limit_bytes=40 * 1024 * 1024),
    )(p)


WIDE = 640


MESH_ID = pl.DeviceIdType.MESH


def place():
    f = lax.axis_index("fsdp")
    return f // 8, (f // 2) % 4, f % 2


def to_device(x, z, core):
    return {"fsdp": (x * 4 + z) * 2 + core}


def greet(peers):
    barrier = pltpu.get_barrier_semaphore()
    for peer in peers:
        pl.semaphore_signal(barrier, inc=1, device_id=peer, device_id_type=MESH_ID)
    pl.semaphore_wait(barrier, len(peers))


def remote(src, dst, sends, recvs, index, peer):
    return pltpu.make_async_remote_copy(
        src_ref=src,
        dst_ref=dst,
        send_sem=sends.at[index],
        recv_sem=recvs.at[index],
        device_id=peer,
        device_id_type=MESH_ID,
    )


def rows_at(start, count):
    return pl.ds(pl.multiple_of(start, count), count)


def start_all(copies):
    for copy in copies:
        copy.start()


def wait_recv_all(copies):
    for copy in copies:
        copy.wait_recv()


def gradient_body(scale, act, grads, lf, rf, g, fac, act2, flip, part, sent_c, got_c, sent_x, got_x, acc_x, sent_z, got_z, sent_f, twice, sends, recvs):
    x, z, core = place()
    tensor = lax.axis_index("tensor")
    partner = to_device(x, z, 1 - core)
    peers_x = [to_device((x + d) % 4, z, core) for d in (1, 2, 3)]
    peers_z = [to_device(x, (z + d) % 4, core) for d in (1, 2, 3)]
    other = {"tensor": 1 - tensor}
    greet([partner, other] + peers_x + peers_z)
    started = []

    def launch(copies):
        start_all(copies)
        started.extend(copies)
        return copies

    swap = launch([remote(act, act2, sends, recvs, 0, other)])
    chip = (x * 4 + z) * 64

    near = pl.ds(pl.multiple_of(chip // 128 * 128, 128), WIDE)

    def pack(factor):
        narrow = factor[...].astype(jnp.bfloat16)
        twice[:, :N] = narrow
        twice[:, N:] = narrow
        return twice[:, near]

    @pl.when(core == 0)
    def _():
        fac[rows_at(chip, 32), :] = pack(lf)
        sent_f[...] = pack(rf)

    @pl.when(core == 1)
    def _():
        fac[rows_at(chip + 32, 32), :] = pack(rf)
        sent_f[...] = pack(lf)

    fac_c = launch([remote(sent_f, fac.at[rows_at(chip + core * 32, 32)], sends, recvs, 1, partner)])

    def multiply(o, source):
        flip[...] = source[...].T
        sent_c[o] = nn(flip[rows_at((1 - core) * 256, 256), :], grads[...]).astype(jnp.bfloat16)
        copies = launch([remote(sent_c.at[o], got_c.at[o], sends, recvs, 2 + o, partner)])
        part[o] = nn(flip[rows_at(core * 256, 256), :], grads[...])
        return copies

    def reduce_x(o, copies):
        wait_recv_all(copies)
        part[o] += got_c[o].astype(jnp.float32)
        for d in (1, 2, 3):
            sent_x[o, d - 1] = part[o, rows_at((x + d) % 4 * 64, 64), :].astype(jnp.bfloat16)
        return launch([
            remote(sent_x.at[o, d], got_x.at[o, d], sends, recvs, 4 + o * 3 + d, peers_x[d]) for d in range(3)
        ])

    def reduce_z(o, copies):
        wait_recv_all(copies)
        total = part[o, rows_at(x * 64, 64), :]
        for d in range(3):
            total += got_x[o, d].astype(jnp.float32)
        acc_x[o] = total
        for d in (1, 2, 3):
            sent_z[o, d - 1] = acc_x[o, rows_at((z + d) % 4 * 16, 16), :].astype(jnp.bfloat16)
        return launch([
            remote(sent_z.at[o, d], got_z.at[o, d], sends, recvs, 10 + o * 3 + d, peers_z[d]) for d in range(3)
        ])

    def base(o):
        half = tensor if o == 0 else 1 - tensor
        return half * 512 + core * 256

    def gather_z(o, copies):
        wait_recv_all(copies)
        total = acc_x[o, rows_at(z * 16, 16), :]
        for d in range(3):
            total += got_z[o, d].astype(jnp.float32)
        mine = rows_at(base(o) + x * 64 + z * 16, 16)
        g[mine, :] = (total * scale).astype(jnp.bfloat16)
        return launch([remote(g.at[mine], g.at[mine], sends, recvs, 16 + o * 3 + d, peers_z[d]) for d in range(3)])

    def gather_x(o, copies):
        wait_recv_all(copies)
        mine = rows_at(base(o) + x * 64, 64)
        return launch([remote(g.at[mine], g.at[mine], sends, recvs, 22 + o * 3 + d, peers_x[d]) for d in range(3)])

    def gather_c(o, copies):
        wait_recv_all(copies)
        mine = rows_at(base(o), 256)
        return launch([remote(g.at[mine], g.at[mine], sends, recvs, 28 + o, partner)])

    c0 = multiply(0, act)
    x0 = reduce_x(0, c0)
    z0 = reduce_z(0, x0)
    wait_recv_all(fac_c)
    mine_z = rows_at(chip, 64)
    fac_z = launch([remote(fac.at[mine_z], fac.at[mine_z], sends, recvs, 30 + d, peers_z[d]) for d in range(3)])
    wait_recv_all(swap)
    c1 = multiply(1, act2)
    gz0 = gather_z(0, z0)
    x1 = reduce_x(1, c1)
    wait_recv_all(fac_z)
    mine_x = rows_at(x * 256, 256)
    fac_x = launch([remote(fac.at[mine_x], fac.at[mine_x], sends, recvs, 33 + d, peers_x[d]) for d in range(3)])
    gx0 = gather_x(0, gz0)
    z1 = reduce_z(1, x1)
    gz1 = gather_z(1, z1)
    gx1 = gather_x(1, gz1)
    gc0 = gather_c(0, gx0)
    gc1 = gather_c(1, gx1)
    wait_recv_all(gc0)
    wait_recv_all(fac_x)
    wait_recv_all(gc1)
    for copy in started:
        copy.wait_send()


def summed_gradient(activations, out_grads, lf, rf, scale):
    bf, f32 = jnp.bfloat16, jnp.float32
    vm = pl.BlockSpec(memory_space=pltpu.VMEM)
    return pl.pallas_call(
        functools.partial(gradient_body, scale),
        out_shape=(jax.ShapeDtypeStruct((N, N), bf), jax.ShapeDtypeStruct((N, WIDE), bf)),
        in_specs=[vm] * 4,
        out_specs=(vm,) * 2,
        scratch_shapes=[
            pltpu.VMEM((512, 512), bf),
            pltpu.VMEM((512, 512), bf),
            pltpu.VMEM((2, 256, N), f32),
            pltpu.VMEM((2, 256, N), bf),
            pltpu.VMEM((2, 256, N), bf),
            pltpu.VMEM((2, 3, 64, N), bf),
            pltpu.VMEM((2, 3, 64, N), bf),
            pltpu.VMEM((2, 64, N), f32),
            pltpu.VMEM((2, 3, 16, N), bf),
            pltpu.VMEM((2, 3, 16, N), bf),
            pltpu.VMEM((32, WIDE), bf),
            pltpu.VMEM((32, 2 * N), bf),
            pltpu.SemaphoreType.DMA((36,)),
            pltpu.SemaphoreType.DMA((36,)),
        ],
        compiler_params=pltpu.CompilerParams(
            collective_id=0, has_side_effects=True, vmem_limit_bytes=40 * 1024 * 1024
        ),
        name="summed_gradient",
    )(activations, out_grads, lf, rf)


def mixed_dot(left, right):
    return jnp.dot(left, right, preferred_element_type=jnp.float32)


def pair(x):
    hi = lax.reduce_precision(x, 8, 7)
    return hi.astype(jnp.bfloat16), (x - hi).astype(jnp.bfloat16)


def two_pass(wide, narrow):
    rows = wide.shape[0]
    both = mixed_dot(jnp.concatenate(pair(wide), 0), narrow)
    return both[:rows] + both[rows:]


def blocked_cholesky(grams):
    order = grams.shape[-1]
    half = order // 2
    upper_left = grams[:, :half, :half]
    lower_left = grams[:, half:, :half]
    lower_right = grams[:, half:, half:]
    head = jnp.linalg.cholesky(upper_left)
    panel_t = jax.scipy.linalg.solve_triangular(head, jnp.swapaxes(lower_left, 1, 2), lower=True)
    panel = jnp.swapaxes(panel_t, 1, 2)
    schur = lower_right - jnp.einsum("bik,bjk->bij", panel, panel, precision=lax.Precision.HIGHEST)
    tail = jnp.linalg.cholesky(schur)
    zeros_block = jnp.zeros_like(lower_left)
    top = jnp.concatenate([head, jnp.swapaxes(zeros_block, 1, 2)], axis=2)
    bottom = jnp.concatenate([panel, tail], axis=2)
    return jnp.concatenate([top, bottom], axis=1)


def whole_factor(near):
    tiles = [[None] * 8 for _ in range(8)]
    for b in range(8):
        for k in range(5):
            tile = near[b * 128:(b + 1) * 128, k * 128:(k + 1) * 128]
            tiles[b][(b + k) % 8] = tile
            if 0 < k < 4:
                tiles[(b + k) % 8][b] = tile.T
    return jnp.concatenate([jnp.concatenate(row, 1) for row in tiles], 0).astype(jnp.float32)


def exact_orth(power):
    lower = blocked_cholesky(mixed_dot(power.T, power)[None])[0]
    solved = jax.scipy.linalg.solve_triangular(lower, power.T.astype(jnp.float32), lower=True)
    return solved.T.astype(jnp.bfloat16)


def orthonormal(power):
    quick, residual = orth(power)
    return lax.cond(residual[0, 0] < RESIDUAL_LIMIT, lambda: quick, lambda: exact_orth(power))


def per_device(
    activations,
    out_grads,
    moment,
    moment_sq,
    left_factor,
    right_factor,
    left_basis,
    right_basis,
    params,
    anchor,
    outer_momentum,
):
    owners = lax.axis_size("fsdp")
    row_count = left_factor.shape[2]
    block_width = left_factor.shape[3]
    grad_scale = 1.0 / math.sqrt(activations.shape[1] * owners)
    core = lax.axis_index("fsdp") % 2
    first_row = lax.axis_index("fsdp") * row_count
    gradient_full, near_columns = summed_gradient(
        activations[0], out_grads[0], left_factor[0, 0], right_factor[0, 0], grad_scale
    )
    own_rows = lax.dynamic_slice_in_dim(gradient_full, first_row, row_count, 0)
    left_old = left_basis[0, 0]
    right_old = right_basis[0, 0]
    left_columns = lax.dynamic_slice_in_dim(left_old, first_row, row_count, 1)
    half_turn = mixed_dot(left_columns.T, gradient_full).astype(jnp.bfloat16)
    rotated = mixed_dot(half_turn, right_old)
    first_moment = BETA_ONE * moment[0, 0] + (1.0 - BETA_ONE) * rotated
    second_moment = BETA_TWO * moment_sq[0, 0] + (1.0 - BETA_TWO) * rotated * rotated
    normed = (first_moment / (jnp.sqrt(second_moment) + ADAM_EPS)).astype(jnp.bfloat16)
    own_columns = lax.dynamic_slice_in_dim(gradient_full, first_row, row_count, 1)
    left_next = (
        FACTOR_BETA * left_factor[0, 0]
        + (1.0 - FACTOR_BETA) * mixed_dot(own_rows, gradient_full.T) / block_width
    )
    right_next = (
        FACTOR_BETA * right_factor[0, 0]
        + (1.0 - FACTOR_BETA) * mixed_dot(own_columns.T, gradient_full) / block_width
    )
    oriented = jnp.where(core == 0, gradient_full, gradient_full.T)
    factor_next = (
        FACTOR_BETA * whole_factor(near_columns)
        + (1.0 - FACTOR_BETA) * mixed_dot(oriented, oriented.T) / block_width
    )
    power = mixed_dot(
        factor_next.astype(jnp.bfloat16), jnp.where(core == 0, left_old, right_old)
    ).astype(jnp.bfloat16)
    normed_all = lax.all_gather(normed, "fsdp", axis=0, tiled=True)
    first_all = lax.all_gather(first_moment, "fsdp", axis=0, tiled=True)
    mine = orthonormal(power)
    other = lax.ppermute(mine, "fsdp", [(d, d ^ 1) for d in range(owners)])
    left_new = jnp.where(core == 0, mine, other)
    right_new = jnp.where(core == 0, other, mine)
    left_rows = lax.dynamic_slice_in_dim(left_old, first_row, row_count, 0)
    back_half = mixed_dot(left_rows, normed_all).astype(jnp.bfloat16)
    update = mixed_dot(back_half, right_old.T)
    new_columns = lax.dynamic_slice_in_dim(left_new, first_row, row_count, 1)
    turn_rows = mixed_dot(new_columns.T, left_old)
    high_first, low_first = pair(first_all)
    moment_next = two_pass(turn_rows, high_first) + mixed_dot(turn_rows.astype(jnp.bfloat16), low_first)
    moment_next = two_pass(two_pass(moment_next, right_old.T), right_new)
    island_delta = anchor[0] - (params[0, 0] - INNER_RATE * update)
    average = lax.psum(island_delta, "island") / lax.axis_size("island")
    momentum_next = OUTER_MOMENT * outer_momentum[0] + average
    anchor_next = anchor[0] - OUTER_RATE * (average + OUTER_MOMENT * momentum_next)
    return (
        anchor_next[None],
        momentum_next[None],
        moment_next[None, None],
        second_moment[None, None],
        left_next[None, None],
        right_next[None, None],
        left_new[None, None],
        right_new[None, None],
    )


def solution(mesh):
    in_specs = (
        P("island", "fsdp", "tensor"),
        P("island", "fsdp", "tensor"),
        P("island", "tensor", "fsdp", None),
        P("island", "tensor", "fsdp", None),
        P("island", "tensor", "fsdp", None),
        P("island", "tensor", "fsdp", None),
        P("island", "tensor", None, None),
        P("island", "tensor", None, None),
        P("island", "tensor", "fsdp", None),
        P("tensor", "fsdp", None),
        P("tensor", "fsdp", None),
    )
    out_specs = (
        P("tensor", "fsdp", None),
        P("tensor", "fsdp", None),
        P("island", "tensor", "fsdp", None),
        P("island", "tensor", "fsdp", None),
        P("island", "tensor", "fsdp", None),
        P("island", "tensor", "fsdp", None),
        P("island", "tensor", None, None),
        P("island", "tensor", None, None),
    )
    return jax.shard_map(
        per_device, mesh=mesh, in_specs=in_specs, out_specs=out_specs, check_vma=False
    )
```

```python
import functools
import math

import jax
import jax.numpy as jnp
from jax import lax
from jax.experimental import pallas as pl
from jax.experimental.pallas import tpu as pltpu
from jax.sharding import PartitionSpec as P

BETA_ONE = 0.9
BETA_TWO = 0.95
FACTOR_BETA = 0.9
ADAM_EPS = 1e-08
INNER_RATE = 0.5
OUTER_RATE = 0.7
OUTER_MOMENT = 0.9
RESIDUAL_LIMIT = 0.06

N = 1024
H = 512
Q4 = 256
ROUGH = 4


def nn(a, b):
    return jnp.dot(a, b, preferred_element_type=jnp.float32)


def nt(a, b):
    return lax.dot_general(a, b, (((1,), (1,)), ((), ())), preferred_element_type=jnp.float32)


def split(x):
    hi = x.astype(jnp.bfloat16)
    return hi, (x - hi.astype(jnp.float32)).astype(jnp.bfloat16)


def nt3(a, b):
    return nt(a[0], b[0]) + (nt(a[0], b[1]) + nt(a[1], b[0]))


def nn3(a, b):
    return nn(a[0], b[0]) + (nn(a[0], b[1]) + nn(a[1], b[0]))


def iotas(n):
    return lax.broadcasted_iota(jnp.int32, (n, n), 0), lax.broadcasted_iota(jnp.int32, (n, n), 1)


def low(e):
    r, c = iotas(e.shape[0])
    return jnp.where(r > c, e, jnp.where(r == c, 0.5 * e, 0.0))


def minus_eye(e):
    r, c = iotas(e.shape[0])
    return jnp.where(r == c, e - 1.0, e)


def diag_rows(s):
    r, c = iotas(s.shape[0])
    picked = jnp.where(r == c, s, 0.0)
    return jnp.sum(picked, 1, keepdims=True), jnp.sum(picked, 0, keepdims=True)


def residual(x, s, y_ref):
    a, b = slice(0, Q4), slice(Q4, H)
    if len(x) == 1:
        xa, x2 = x[0][a, a], x[0][b, :]
        ya = nn(xa, s[0][a, a]).astype(jnp.bfloat16)
        y2 = nn(x2, s[0][...]).astype(jnp.bfloat16)
        return nt(ya, xa), nt(y2[:, a], xa), nt(y2, x2)
    xa = (x[0][a, a], x[1][a, a])
    x2 = (x[0][b, :], x[1][b, :])
    ya = split(nn3(xa, (s[0][a, a], s[1][a, a])))
    y2 = split(nn3(x2, (s[0][...], s[1][...])))
    y2a = (y2[0][:, a], y2[1][:, a])
    return nt3(ya, xa), nt3(y2a, xa), nt3(y2, x2)


def leaf(s_ref, x_ref, sh, sl, xh, xl):
    a, b = slice(0, Q4), slice(Q4, H)
    dc, dr = diag_rows(s_ref[...])
    dc, dr = lax.rsqrt(dc), lax.rsqrt(dr)
    sn = s_ref[...] * dc * dr
    hi, lo = split(sn)
    sh[...] = hi
    sl[...] = lo
    e0 = minus_eye(sn)
    f0 = low(e0)
    r, c = iotas(H)
    x0 = jnp.where(r == c, 1.0 - f0, -f0)
    x_ref[...] = x0
    xh[...] = x0.astype(jnp.bfloat16)

    def update(e, fine):
        eaa, eca, edd = e
        faa, fdd = low(eaa).astype(jnp.bfloat16), low(edd).astype(jnp.bfloat16)
        fca = eca.astype(jnp.bfloat16)
        xa, xc, xd = xh[a, a], xh[b, a], xh[b, b]
        na = x_ref[a, a] - nn(faa, xa)
        nc = x_ref[b, a] - (nn(fca, xa) + nn(fdd, xc))
        nd = x_ref[b, b] - nn(fdd, xd)
        x_ref[a, a] = na
        x_ref[b, a] = nc
        x_ref[b, b] = nd
        if not fine:
            xh[a, a] = na.astype(jnp.bfloat16)
            xh[b, a] = nc.astype(jnp.bfloat16)
            xh[b, b] = nd.astype(jnp.bfloat16)

    def step(_, carry):
        eaa, eca, edd = residual((xh,), (sh,), None)
        update((minus_eye(eaa), eca, minus_eye(edd)), False)
        return carry

    lax.fori_loop(0, ROUGH, step, 0)
    hi, lo = split(x_ref[...])
    xh[...] = hi
    xl[...] = lo
    eaa, eca, edd = residual((xh, xl), (sh, sl), None)
    eaa, edd = minus_eye(eaa), minus_eye(edd)
    left = jnp.sum(eaa * eaa) + 2.0 * jnp.sum(eca * eca) + jnp.sum(edd * edd)
    update((eaa, eca, edd), True)
    x_ref[...] = x_ref[...] * dr
    hi, lo = split(x_ref[...])
    xh[...] = hi
    xl[...] = lo
    return left


WIDE = 640


MESH_ID = pl.DeviceIdType.MESH


def place():
    f = lax.axis_index("fsdp")
    return f // 8, (f // 2) % 4, f % 2


def to_device(x, z, core):
    return {"fsdp": (x * 4 + z) * 2 + core}


def greet(peers):
    barrier = pltpu.get_barrier_semaphore()
    for peer in peers:
        pl.semaphore_signal(barrier, inc=1, device_id=peer, device_id_type=MESH_ID)
    pl.semaphore_wait(barrier, len(peers))


def remote(src, dst, sends, recvs, index, peer):
    return pltpu.make_async_remote_copy(
        src_ref=src,
        dst_ref=dst,
        send_sem=sends.at[index],
        recv_sem=recvs.at[index],
        device_id=peer,
        device_id_type=MESH_ID,
    )


def rows_at(start, count):
    return pl.ds(pl.multiple_of(start, count), count)


def start_all(copies):
    for copy in copies:
        copy.start()


def wait_recv_all(copies):
    for copy in copies:
        copy.wait_recv()


def gradient_body(scale, act, grads, lf, rf, g, fac, act2, flip, part, sent_c, got_c, sent_x, got_x, acc_x, sent_z, got_z, sent_f, twice, sends, recvs):
    x, z, core = place()
    tensor = lax.axis_index("tensor")
    partner = to_device(x, z, 1 - core)
    peers_x = [to_device((x + d) % 4, z, core) for d in (1, 2, 3)]
    peers_z = [to_device(x, (z + d) % 4, core) for d in (1, 2, 3)]
    other = {"tensor": 1 - tensor}
    greet([partner, other] + peers_x + peers_z)
    started = []

    def launch(copies):
        start_all(copies)
        started.extend(copies)
        return copies

    swap = launch([remote(act, act2, sends, recvs, 0, other)])
    chip = (x * 4 + z) * 64

    near = pl.ds(pl.multiple_of(chip // 128 * 128, 128), WIDE)

    def pack(factor):
        narrow = factor[...].astype(jnp.bfloat16)
        twice[:, :N] = narrow
        twice[:, N:] = narrow
        return twice[:, near]

    @pl.when(core == 0)
    def _():
        fac[rows_at(chip, 32), :] = pack(lf)
        sent_f[...] = pack(rf)

    @pl.when(core == 1)
    def _():
        fac[rows_at(chip + 32, 32), :] = pack(rf)
        sent_f[...] = pack(lf)

    fac_c = launch([remote(sent_f, fac.at[rows_at(chip + core * 32, 32)], sends, recvs, 1, partner)])

    def multiply(o, source):
        flip[...] = source[...].T
        sent_c[o] = nn(flip[rows_at((1 - core) * 256, 256), :], grads[...]).astype(jnp.bfloat16)
        copies = launch([remote(sent_c.at[o], got_c.at[o], sends, recvs, 2 + o, partner)])
        part[o] = nn(flip[rows_at(core * 256, 256), :], grads[...])
        return copies

    def reduce_x(o, copies):
        wait_recv_all(copies)
        part[o] += got_c[o].astype(jnp.float32)
        for d in (1, 2, 3):
            sent_x[o, d - 1] = part[o, rows_at((x + d) % 4 * 64, 64), :].astype(jnp.bfloat16)
        return launch([
            remote(sent_x.at[o, d], got_x.at[o, d], sends, recvs, 4 + o * 3 + d, peers_x[d]) for d in range(3)
        ])

    def reduce_z(o, copies):
        wait_recv_all(copies)
        total = part[o, rows_at(x * 64, 64), :]
        for d in range(3):
            total += got_x[o, d].astype(jnp.float32)
        acc_x[o] = total
        for d in (1, 2, 3):
            sent_z[o, d - 1] = acc_x[o, rows_at((z + d) % 4 * 16, 16), :].astype(jnp.bfloat16)
        return launch([
            remote(sent_z.at[o, d], got_z.at[o, d], sends, recvs, 10 + o * 3 + d, peers_z[d]) for d in range(3)
        ])

    def base(o):
        half = tensor if o == 0 else 1 - tensor
        return half * 512 + core * 256

    def gather_z(o, copies):
        wait_recv_all(copies)
        total = acc_x[o, rows_at(z * 16, 16), :]
        for d in range(3):
            total += got_z[o, d].astype(jnp.float32)
        mine = rows_at(base(o) + x * 64 + z * 16, 16)
        g[mine, :] = (total * scale).astype(jnp.bfloat16)
        return launch([remote(g.at[mine], g.at[mine], sends, recvs, 16 + o * 3 + d, peers_z[d]) for d in range(3)])

    def gather_x(o, copies):
        wait_recv_all(copies)
        mine = rows_at(base(o) + x * 64, 64)
        return launch([remote(g.at[mine], g.at[mine], sends, recvs, 22 + o * 3 + d, peers_x[d]) for d in range(3)])

    def gather_c(o, copies):
        wait_recv_all(copies)
        mine = rows_at(base(o), 256)
        return launch([remote(g.at[mine], g.at[mine], sends, recvs, 28 + o, partner)])

    c0 = multiply(0, act)
    x0 = reduce_x(0, c0)
    z0 = reduce_z(0, x0)
    wait_recv_all(fac_c)
    mine_z = rows_at(chip, 64)
    fac_z = launch([remote(fac.at[mine_z], fac.at[mine_z], sends, recvs, 30 + d, peers_z[d]) for d in range(3)])
    wait_recv_all(swap)
    c1 = multiply(1, act2)
    gz0 = gather_z(0, z0)
    x1 = reduce_x(1, c1)
    wait_recv_all(fac_z)
    mine_x = rows_at(x * 256, 256)
    fac_x = launch([remote(fac.at[mine_x], fac.at[mine_x], sends, recvs, 33 + d, peers_x[d]) for d in range(3)])
    gx0 = gather_x(0, gz0)
    z1 = reduce_z(1, x1)
    gz1 = gather_z(1, z1)
    gx1 = gather_x(1, gz1)
    gc0 = gather_c(0, gx0)
    gc1 = gather_c(1, gx1)
    wait_recv_all(gc0)
    wait_recv_all(fac_x)
    wait_recv_all(gc1)
    for copy in started:
        copy.wait_send()


def summed_gradient(activations, out_grads, lf, rf, scale):
    bf, f32 = jnp.bfloat16, jnp.float32
    vm = pl.BlockSpec(memory_space=pltpu.VMEM)
    return pl.pallas_call(
        functools.partial(gradient_body, scale),
        out_shape=(jax.ShapeDtypeStruct((N, N), bf), jax.ShapeDtypeStruct((N, WIDE), bf)),
        in_specs=[vm] * 4,
        out_specs=(vm,) * 2,
        scratch_shapes=[
            pltpu.VMEM((512, 512), bf),
            pltpu.VMEM((512, 512), bf),
            pltpu.VMEM((2, 256, N), f32),
            pltpu.VMEM((2, 256, N), bf),
            pltpu.VMEM((2, 256, N), bf),
            pltpu.VMEM((2, 3, 64, N), bf),
            pltpu.VMEM((2, 3, 64, N), bf),
            pltpu.VMEM((2, 64, N), f32),
            pltpu.VMEM((2, 3, 16, N), bf),
            pltpu.VMEM((2, 3, 16, N), bf),
            pltpu.VMEM((32, WIDE), bf),
            pltpu.VMEM((32, 2 * N), bf),
            pltpu.SemaphoreType.DMA((36,)),
            pltpu.SemaphoreType.DMA((36,)),
        ],
        compiler_params=pltpu.CompilerParams(
            collective_id=0, has_side_effects=True, vmem_limit_bytes=40 * 1024 * 1024
        ),
        name="summed_gradient",
    )(activations, out_grads, lf, rf)


def refresh_body(
    g, fac, lb, rb, mom, msq, lf, rf, par, anc, om,
    left_out, right_out, p_own, p_other, first_all,
    moment_out, msq_out, left_next, right_next, anchor_out, momentum_out, res_out,
    turned, seen, out32, whole, gm, bo, p_ref, pt, q_ref, q_got, fx, keep, kept, upd, isl, mrows, res_own, res_got,
    s_ref, a21, x_ref, sh, sl, xh, xl, l21h, l21l, sends, recvs, local,
):
    bf, f32 = jnp.bfloat16, jnp.float32
    fsdp, island = lax.axis_index("fsdp"), lax.axis_index("island")
    x, z, core = place()
    partner = to_device(x, z, 1 - core)
    peers_x = [to_device((x + d) % 4, z, core) for d in (1, 2, 3)]
    peers_z = [to_device(x, (z + d) % 4, core) for d in (1, 2, 3)]
    peers_y = [{"island": (island + d) % 4} for d in (1, 2, 3)]
    chip = (x * 4 + z) * 64
    f, h = slice(0, H), slice(H, N)
    a, b = slice(0, Q4), slice(Q4, H)
    greet([partner] + peers_x + peers_z + peers_y)
    started = []

    def launch(copies):
        start_all(copies)
        started.extend(copies)
        return copies

    def tile(i):
        return rows_at(i * Q4, Q4)

    turned[...] = lb[:, pl.ds(pl.multiple_of(fsdp // 4 * 128, 128), 128)].T
    half = nn(turned[rows_at(fsdp % 4 * 32, 32), :], g[...]).astype(bf)
    rotated = nn(half, rb[...])
    first = BETA_ONE * mom[...] + (1.0 - BETA_ONE) * rotated
    second = BETA_TWO * msq[...] + (1.0 - BETA_TWO) * rotated * rotated
    msq_out[...] = second
    normed = (first / (jnp.sqrt(second) + ADAM_EPS)).astype(bf)
    first = first.astype(bf)

    @pl.when(core == 0)
    def _():
        seen[rows_at(chip, 32), :] = normed
        out32[...] = first
        gm[...] = g[...]
        bo[...] = lb[...]

    @pl.when(core == 1)
    def _():
        seen[rows_at(chip + 32, 32), :] = first
        out32[...] = normed
        gm[...] = g[...].T
        bo[...] = rb[...]

    seen_c = launch([remote(out32, seen.at[rows_at(chip + core * 32, 32)], sends, recvs, 0, partner)])

    for i in range(8):
        for k in range(5):
            j = (i + k) % 8
            block = fac[i * 128:(i + 1) * 128, k * 128:(k + 1) * 128]
            whole[i * 128:(i + 1) * 128, j * 128:(j + 1) * 128] = block
            if 0 < k < 4:
                whole[j * 128:(j + 1) * 128, i * 128:(i + 1) * 128] = block.T

    wait_recv_all(seen_c)
    mine = rows_at(chip, 64)
    seen_z = launch([remote(seen.at[mine], seen.at[mine], sends, recvs, 1 + d, peers_z[d]) for d in range(3)])

    def power_rows(i, c):
        fx[...] = nt(gm[tile(i), :], gm[...]) * ((1.0 - FACTOR_BETA) / N)

        @pl.when(i == x)
        def _():
            keep[...] = fx[rows_at(z * 64, 64), :]

        nxt = (FACTOR_BETA * whole[tile(i), :].astype(f32) + fx[...]).astype(bf)
        p_ref[tile(i), :] = nn(nxt, bo[...]).astype(bf)
        return c

    lax.fori_loop(0, 4, power_rows, 0)
    p_copy = pltpu.make_async_copy(p_ref, p_own, local.at[0])
    p_copy.start()
    p_swap = launch([remote(p_ref, p_other, sends, recvs, 4, partner)])
    away = rows_at((1 - core) * 32, 32)
    kept_c = launch([remote(keep.at[away], kept, sends, recvs, 5, partner)])

    pt[...] = p_ref[...].T
    s_ref[...] = nt(pt[f, :], pt[f, :])
    a21[...] = nt(pt[h, :], pt[f, :])
    r1 = leaf(s_ref, x_ref, sh, sl, xh, xl)

    wait_recv_all(seen_z)
    mine = rows_at(x * 256, 256)
    seen_x = launch([remote(seen.at[mine], seen.at[mine], sends, recvs, 6 + d, peers_x[d]) for d in range(3)])

    def by_x(t):
        ta = tuple(v[:, a] for v in t)
        xa, x2 = (xh[a, a], xl[a, a]), (xh[b, :], xl[b, :])
        if len(t) == 1:
            return nt(ta[0], xa[0]) + nt(ta[0], xa[1]), nt(t[0], x2[0]) + nt(t[0], x2[1])
        return nt3(ta, xa), nt3(t, x2)

    def l_rows(i, c):
        u, v = by_x(split(a21[tile(i), :]))
        l21h[tile(i), a], l21l[tile(i), a] = split(u)
        l21h[tile(i), b], l21l[tile(i), b] = split(v)
        return c

    lax.fori_loop(0, 2, l_rows, 0)
    s_ref[...] = nt(pt[h, :], pt[h, :]) - nt3((l21h[...], l21l[...]), (l21h[...], l21l[...]))

    def q1_rows(i, c):
        u, v = by_x((p_ref[tile(i), f],))
        q_ref[tile(i), a], pt[tile(i), a] = split(u)
        q_ref[tile(i), b], pt[tile(i), b] = split(v)
        return c

    lax.fori_loop(0, 4, q1_rows, 0)
    q1_swap = launch([remote(q_ref.at[:, pl.ds(0, H)], q_got.at[:, pl.ds(0, H)], sends, recvs, 9, partner)])

    wait_recv_all(kept_c)
    ours, theirs = keep[rows_at(core * 32, 32), :], kept[...]
    left_next[...] = FACTOR_BETA * lf[...] + jnp.where(core == 0, ours, theirs)
    right_next[...] = FACTOR_BETA * rf[...] + jnp.where(core == 0, theirs, ours)

    r2 = leaf(s_ref, x_ref, sh, sl, xh, xl)
    res_own[...] = jnp.full((8, 128), jnp.maximum(r1, r2), f32)
    res_c = launch([remote(res_own, res_got, sends, recvs, 10, partner)])

    wait_recv_all(seen_x)
    upd_c = remote(upd.at[pl.ds(32, 32)], upd.at[pl.ds(32, 32)], sends, recvs, 11, partner)
    first_copy = pltpu.make_async_copy(seen, first_all, local.at[1])
    first_c = remote(seen, first_all, sends, recvs, 12, partner)

    @pl.when(core == 0)
    def _():
        back = nn(lb[rows_at(chip, 64), :], seen[...]).astype(bf)
        upd[...] = nt(back, rb[...])
        upd_c.start()

    @pl.when(core == 1)
    def _():
        first_copy.start()
        first_c.start()

    def q2_rows(i, c):
        t = p_ref[tile(i), h].astype(f32) - nt3((q_ref[tile(i), f], pt[tile(i), f]), (l21h[...], l21l[...]))
        u, v = by_x(split(t))
        q_ref[tile(i), H:H + Q4] = u.astype(bf)
        q_ref[tile(i), H + Q4:N] = v.astype(bf)
        return c

    lax.fori_loop(0, 4, q2_rows, 0)
    q2_swap = launch([remote(q_ref.at[:, pl.ds(H, H)], q_got.at[:, pl.ds(H, H)], sends, recvs, 13, partner)])

    @pl.when(core == 1)
    def _():
        upd_c.wait_recv()

    delta = anc[...] - (par[...] - INNER_RATE * upd[rows_at(core * 32, 32), :])
    isl[island] = delta
    isl_y = launch([remote(isl.at[island], isl.at[island], sends, recvs, 14 + d, peers_y[d]) for d in range(3)])

    wait_recv_all(q1_swap)
    wait_recv_all(q2_swap)

    def outs(flag):
        left, right = (q_ref, q_got) if flag == 0 else (q_got, q_ref)
        return [
            pltpu.make_async_copy(left, left_out, local.at[2]),
            pltpu.make_async_copy(right, right_out, local.at[3]),
        ]

    moment_c = remote(mrows.at[pl.ds(0, 32)], mrows.at[pl.ds(0, 32)], sends, recvs, 17, partner)

    @pl.when(core == 0)
    def _():
        start_all(outs(0))

    @pl.when(core == 1)
    def _():
        start_all(outs(1))

        def twice(v, mm, m):
            both = mm(jnp.concatenate(split(v), 0), m[...])
            return both[:64] + both[64:]

        turned[...] = q_got[:, pl.ds(pl.multiple_of(chip // 128 * 128, 128), 128)].T
        turn = nn(turned[rows_at(chip % 128, 64), :], lb[...])
        mrows[...] = twice(twice(twice(turn, nn, seen), nt, rb), nn, q_ref)
        moment_c.start()

    wait_recv_all(isl_y)
    average = (isl[0] + isl[1] + isl[2] + isl[3]) / 4.0
    momentum = OUTER_MOMENT * om[...] + average
    momentum_out[...] = momentum
    anchor_out[...] = anc[...] - OUTER_RATE * (average + OUTER_MOMENT * momentum)
    wait_recv_all(res_c)
    res_out[...] = jnp.maximum(res_own[...], res_got[...])
    wait_recv_all(p_swap)
    p_copy.wait()

    @pl.when(core == 0)
    def _():
        first_c.wait_recv()
        upd_c.wait_send()
        moment_c.wait_recv()
        for copy in outs(0):
            copy.wait()

    @pl.when(core == 1)
    def _():
        first_copy.wait()
        first_c.wait_send()
        moment_c.wait_send()
        for copy in outs(1):
            copy.wait()

    moment_out[...] = mrows[rows_at(core * 32, 32), :]
    for copy in started:
        copy.wait_send()


def refresh(gradient, near, left_old, right_old, rows):
    bf, f32 = jnp.bfloat16, jnp.float32
    vm, hbm = pl.BlockSpec(memory_space=pltpu.VMEM), pl.BlockSpec(memory_space=pl.ANY)
    square = jax.ShapeDtypeStruct((N, N), bf)
    strip = jax.ShapeDtypeStruct((32, N), f32)
    big = pltpu.VMEM((N, N), bf)
    return pl.pallas_call(
        refresh_body,
        out_shape=(square,) * 5 + (strip,) * 6 + (jax.ShapeDtypeStruct((8, 128), f32),),
        in_specs=[vm] * 11,
        out_specs=(hbm,) * 5 + (vm,) * 7,
        scratch_shapes=[
            pltpu.VMEM((128, N), bf),
            big,
            pltpu.VMEM((32, N), bf),
            big, big, big, big, big, big, big,
            pltpu.VMEM((Q4, N), f32),
            pltpu.VMEM((64, N), f32),
            pltpu.VMEM((32, N), f32),
            pltpu.VMEM((64, N), f32),
            pltpu.VMEM((4, 32, N), f32),
            pltpu.VMEM((64, N), f32),
            pltpu.VMEM((8, 128), f32),
            pltpu.VMEM((8, 128), f32),
            pltpu.VMEM((H, H), f32), pltpu.VMEM((H, H), f32), pltpu.VMEM((H, H), f32),
        ] + [pltpu.VMEM((H, H), bf)] * 6 + [
            pltpu.SemaphoreType.DMA((18,)),
            pltpu.SemaphoreType.DMA((18,)),
            pltpu.SemaphoreType.DMA((4,)),
        ],
        compiler_params=pltpu.CompilerParams(
            collective_id=1, has_side_effects=True, vmem_limit_bytes=54 * 1024 * 1024
        ),
        name="refresh",
    )(gradient, near, left_old, right_old, *rows)


def mixed_dot(left, right):
    return jnp.dot(left, right, preferred_element_type=jnp.float32)


def pair(x):
    hi = lax.reduce_precision(x, 8, 7)
    return hi.astype(jnp.bfloat16), (x - hi).astype(jnp.bfloat16)


def two_pass(wide, narrow):
    rows = wide.shape[0]
    both = mixed_dot(jnp.concatenate(pair(wide), 0), narrow)
    return both[:rows] + both[rows:]


def blocked_cholesky(grams):
    order = grams.shape[-1]
    half = order // 2
    upper_left = grams[:, :half, :half]
    lower_left = grams[:, half:, :half]
    lower_right = grams[:, half:, half:]
    head = jnp.linalg.cholesky(upper_left)
    panel_t = jax.scipy.linalg.solve_triangular(head, jnp.swapaxes(lower_left, 1, 2), lower=True)
    panel = jnp.swapaxes(panel_t, 1, 2)
    schur = lower_right - jnp.einsum("bik,bjk->bij", panel, panel, precision=lax.Precision.HIGHEST)
    tail = jnp.linalg.cholesky(schur)
    zeros_block = jnp.zeros_like(lower_left)
    top = jnp.concatenate([head, jnp.swapaxes(zeros_block, 1, 2)], axis=2)
    bottom = jnp.concatenate([panel, tail], axis=2)
    return jnp.concatenate([top, bottom], axis=1)


def exact_orth(power):
    lower = blocked_cholesky(mixed_dot(power.T, power)[None])[0]
    solved = jax.scipy.linalg.solve_triangular(lower, power.T.astype(jnp.float32), lower=True)
    return solved.T.astype(jnp.bfloat16)


def per_device(
    activations,
    out_grads,
    moment,
    moment_sq,
    left_factor,
    right_factor,
    left_basis,
    right_basis,
    params,
    anchor,
    outer_momentum,
):
    owners = lax.axis_size("fsdp")
    row_count = left_factor.shape[2]
    grad_scale = 1.0 / math.sqrt(activations.shape[1] * owners)
    core = lax.axis_index("fsdp") % 2
    first_row = lax.axis_index("fsdp") * row_count
    left_old, right_old = left_basis[0, 0], right_basis[0, 0]
    gradient, near = summed_gradient(
        activations[0], out_grads[0], left_factor[0, 0], right_factor[0, 0], grad_scale
    )
    rows = (moment, moment_sq, left_factor, right_factor, params)
    rows = tuple(v[0, 0] for v in rows) + (anchor[0], outer_momentum[0])
    (
        left_quick, right_quick, power, power_other, first_all,
        moment_quick, second_moment, left_next, right_next, anchor_next, momentum_next, residual,
    ) = refresh(gradient, near, left_old, right_old, rows)

    def redo(state):
        left_new = exact_orth(jnp.where(core == 0, power, power_other))
        right_new = exact_orth(jnp.where(core == 0, power_other, power))
        new_columns = lax.dynamic_slice_in_dim(left_new, first_row, row_count, 1)
        turned = two_pass(mixed_dot(new_columns.T, left_old), first_all)
        return False, left_new, right_new, two_pass(two_pass(turned, right_old.T), right_new)

    quick = (jnp.logical_not(residual[0, 0] < RESIDUAL_LIMIT), left_quick, right_quick, moment_quick)
    _, left_new, right_new, moment_next = lax.while_loop(lambda state: state[0], redo, quick)
    return (
        anchor_next[None],
        momentum_next[None],
        moment_next[None, None],
        second_moment[None, None],
        left_next[None, None],
        right_next[None, None],
        left_new[None, None],
        right_new[None, None],
    )


def solution(mesh):
    in_specs = (
        P("island", "fsdp", "tensor"),
        P("island", "fsdp", "tensor"),
        P("island", "tensor", "fsdp", None),
        P("island", "tensor", "fsdp", None),
        P("island", "tensor", "fsdp", None),
        P("island", "tensor", "fsdp", None),
        P("island", "tensor", None, None),
        P("island", "tensor", None, None),
        P("island", "tensor", "fsdp", None),
        P("tensor", "fsdp", None),
        P("tensor", "fsdp", None),
    )
    out_specs = (
        P("tensor", "fsdp", None),
        P("tensor", "fsdp", None),
        P("island", "tensor", "fsdp", None),
        P("island", "tensor", "fsdp", None),
        P("island", "tensor", "fsdp", None),
        P("island", "tensor", "fsdp", None),
        P("island", "tensor", None, None),
        P("island", "tensor", None, None),
    )
    return jax.shard_map(
        per_device, mesh=mesh, in_specs=in_specs, out_specs=out_specs, check_vma=False
    )
```

```python
import functools
import math

import jax
import jax.numpy as jnp
from jax import lax
from jax.experimental import pallas as pl
from jax.experimental.pallas import tpu as pltpu
from jax.sharding import PartitionSpec as P

BETA_ONE = 0.9
BETA_TWO = 0.95
FACTOR_BETA = 0.9
ADAM_EPS = 1e-08
INNER_RATE = 0.5
OUTER_RATE = 0.7
OUTER_MOMENT = 0.9
RESIDUAL_LIMIT = 0.06

N = 1024
H = 512
Q4 = 256
ROUGH = 3
VMEM_LIMIT = 58 * 1024 * 1024
FINISH_LIMIT = 60 * 1024 * 1024


def nn(a, b):
    return jnp.dot(a, b, preferred_element_type=jnp.float32)


def nt(a, b):
    return lax.dot_general(a, b, (((1,), (1,)), ((), ())), preferred_element_type=jnp.float32)


def split(x):
    hi = x.astype(jnp.bfloat16)
    return hi, (x - hi.astype(jnp.float32)).astype(jnp.bfloat16)


def nt3(a, b):
    return nt(a[0], b[0]) + (nt(a[0], b[1]) + nt(a[1], b[0]))


def nn3(a, b):
    return nn(a[0], b[0]) + (nn(a[0], b[1]) + nn(a[1], b[0]))


def iotas(n):
    return lax.broadcasted_iota(jnp.int32, (n, n), 0), lax.broadcasted_iota(jnp.int32, (n, n), 1)


def low(e):
    r, c = iotas(e.shape[0])
    return jnp.where(r > c, e, jnp.where(r == c, 0.5 * e, 0.0))


def minus_eye(e):
    r, c = iotas(e.shape[0])
    return jnp.where(r == c, e - 1.0, e)


def diag_rows(s):
    r, c = iotas(s.shape[0])
    picked = jnp.where(r == c, s, 0.0)
    return jnp.sum(picked, 1, keepdims=True), jnp.sum(picked, 0, keepdims=True)


def residual(x, s, y_ref):
    a, b = slice(0, Q4), slice(Q4, H)
    if len(x) == 1:
        xa, x2 = x[0][a, a], x[0][b, :]
        ya = nn(xa, s[0][a, a]).astype(jnp.bfloat16)
        y2 = nn(x2, s[0][...]).astype(jnp.bfloat16)
        return nt(ya, xa), nt(y2[:, a], xa), nt(y2, x2)
    xa = (x[0][a, a], x[1][a, a])
    x2 = (x[0][b, :], x[1][b, :])
    ya = split(nn3(xa, (s[0][a, a], s[1][a, a])))
    y2 = split(nn3(x2, (s[0][...], s[1][...])))
    y2a = (y2[0][:, a], y2[1][:, a])
    return nt3(ya, xa), nt3(y2a, xa), nt3(y2, x2)


def leaf(s_ref, x_ref, sh, sl, xh, xl):
    a, b = slice(0, Q4), slice(Q4, H)
    dc, dr = diag_rows(s_ref[...])
    dc, dr = lax.rsqrt(dc), lax.rsqrt(dr)
    sn = s_ref[...] * dc * dr
    hi, lo = split(sn)
    sh[...] = hi
    sl[...] = lo
    e0 = minus_eye(sn)
    f0 = low(e0)
    r, c = iotas(H)
    x0 = jnp.where(r == c, 1.0 - f0, -f0)
    x_ref[...] = x0
    xh[...] = x0.astype(jnp.bfloat16)

    def update(e, fine):
        eaa, eca, edd = e
        faa, fdd = low(eaa).astype(jnp.bfloat16), low(edd).astype(jnp.bfloat16)
        fca = eca.astype(jnp.bfloat16)
        xa, xc, xd = xh[a, a], xh[b, a], xh[b, b]
        na = x_ref[a, a] - nn(faa, xa)
        nc = x_ref[b, a] - (nn(fca, xa) + nn(fdd, xc))
        nd = x_ref[b, b] - nn(fdd, xd)
        x_ref[a, a] = na
        x_ref[b, a] = nc
        x_ref[b, b] = nd
        if not fine:
            xh[a, a] = na.astype(jnp.bfloat16)
            xh[b, a] = nc.astype(jnp.bfloat16)
            xh[b, b] = nd.astype(jnp.bfloat16)

    def step(_, carry):
        eaa, eca, edd = residual((xh,), (sh,), None)
        update((minus_eye(eaa), eca, minus_eye(edd)), False)
        return carry

    lax.fori_loop(0, ROUGH, step, 0)
    hi, lo = split(x_ref[...])
    xh[...] = hi
    xl[...] = lo
    eaa, eca, edd = residual((xh, xl), (sh, sl), None)
    eaa, edd = minus_eye(eaa), minus_eye(edd)
    left = jnp.sum(eaa * eaa) + 2.0 * jnp.sum(eca * eca) + jnp.sum(edd * edd)
    update((eaa, eca, edd), True)
    x_ref[...] = x_ref[...] * dr
    hi, lo = split(x_ref[...])
    xh[...] = hi
    xl[...] = lo
    return left


WIDE = 640


MESH_ID = pl.DeviceIdType.MESH


def place():
    f = lax.axis_index("fsdp")
    return f // 8, (f // 2) % 4, f % 2


def to_device(x, z, core):
    return {"fsdp": (x * 4 + z) * 2 + core}


def greet(peers):
    barrier = pltpu.get_barrier_semaphore()
    for peer in peers:
        pl.semaphore_signal(barrier, inc=1, device_id=peer, device_id_type=MESH_ID)
    pl.semaphore_wait(barrier, len(peers))


def remote(src, dst, sends, recvs, index, peer):
    return pltpu.make_async_remote_copy(
        src_ref=src,
        dst_ref=dst,
        send_sem=sends.at[index],
        recv_sem=recvs.at[index],
        device_id=peer,
        device_id_type=MESH_ID,
    )


def rows_at(start, count):
    return pl.ds(pl.multiple_of(start, count), count)


def start_all(copies):
    for copy in copies:
        copy.start()


def wait_recv_all(copies):
    for copy in copies:
        copy.wait_recv()


def step_body(
    scale, act_in, grads_in, lf_in, rf_in, mom_in, msq_in, lb_in, rb_in, par_in, anc_in, om_in,
    p_own, p_other, mine_out, got_out, first_all,
    msq_out, left_next, right_next, anchor_out, momentum_out, res_out,
    act, grads, lf, rf, mom, msq, lb, rb, par, anc, om,
    g, fac, act2, flip, part, sent_c, got_c, sent_x, got_x, acc_x, sent_z, got_z, sent_f, twice,
    turned, seen, out32, whole, gm, bo, ff, p_ref, pt, q_ref, kept, upd, isl, res_own, res_got,
    s_ref, a21, x_ref, sh, sl, xh, xl, l21h, l21l, sends, recvs, local,
):
    bf, f32 = jnp.bfloat16, jnp.float32
    pairs = (
        (act_in, act), (grads_in, grads), (lf_in, lf), (rf_in, rf), (mom_in, mom), (msq_in, msq),
        (lb_in, lb), (rb_in, rb), (par_in, par), (anc_in, anc), (om_in, om),
    )
    loads = [pltpu.make_async_copy(src, dst, local.at[i]) for i, (src, dst) in enumerate(pairs)]
    start_all(loads)

    def arrive(i):
        loads[i].wait()

    fsdp, island, tensor = lax.axis_index("fsdp"), lax.axis_index("island"), lax.axis_index("tensor")
    x, z, core = place()
    partner = to_device(x, z, 1 - core)
    peers_x = [to_device((x + d) % 4, z, core) for d in (1, 2, 3)]
    peers_z = [to_device(x, (z + d) % 4, core) for d in (1, 2, 3)]
    peers_y = [{"island": (island + d) % 4} for d in (1, 2, 3)]
    other = {"tensor": 1 - tensor}
    chip = (x * 4 + z) * 64
    f, h = slice(0, H), slice(H, N)
    a, b = slice(0, Q4), slice(Q4, H)
    greet([partner, other] + peers_x + peers_z + peers_y)
    started = []

    def launch(copies):
        start_all(copies)
        started.extend(copies)
        return copies

    def tile(i):
        return rows_at(i * Q4, Q4)

    arrive(0)
    swap = launch([remote(act, act2, sends, recvs, 0, other)])

    arrive(2)
    arrive(3)
    near = pl.ds(pl.multiple_of(chip // 128 * 128, 128), WIDE)

    def pack(factor):
        narrow = factor[...].astype(jnp.bfloat16)
        twice[:, :N] = narrow
        twice[:, N:] = narrow
        return twice[:, near]

    @pl.when(core == 0)
    def _():
        fac[rows_at(chip, 32), :] = pack(lf)
        sent_f[...] = pack(rf)

    @pl.when(core == 1)
    def _():
        fac[rows_at(chip + 32, 32), :] = pack(rf)
        sent_f[...] = pack(lf)

    fac_c = launch([remote(sent_f, fac.at[rows_at(chip + core * 32, 32)], sends, recvs, 1, partner)])

    def multiply(o, source):
        flip[...] = source[...].T
        sent_c[o] = nn(flip[rows_at((1 - core) * 256, 256), :], grads[...]).astype(jnp.bfloat16)
        copies = launch([remote(sent_c.at[o], got_c.at[o], sends, recvs, 2 + o, partner)])
        part[o] = nn(flip[rows_at(core * 256, 256), :], grads[...])
        return copies

    def reduce_x(o, copies):
        wait_recv_all(copies)
        part[o] += got_c[o].astype(jnp.float32)
        for d in (1, 2, 3):
            sent_x[o, d - 1] = part[o, rows_at((x + d) % 4 * 64, 64), :].astype(jnp.bfloat16)
        return launch([
            remote(sent_x.at[o, d], got_x.at[o, d], sends, recvs, 4 + o * 3 + d, peers_x[d]) for d in range(3)
        ])

    def reduce_z(o, copies):
        wait_recv_all(copies)
        total = part[o, rows_at(x * 64, 64), :]
        for d in range(3):
            total += got_x[o, d].astype(jnp.float32)
        acc_x[o] = total
        for d in (1, 2, 3):
            sent_z[o, d - 1] = acc_x[o, rows_at((z + d) % 4 * 16, 16), :].astype(jnp.bfloat16)
        return launch([
            remote(sent_z.at[o, d], got_z.at[o, d], sends, recvs, 10 + o * 3 + d, peers_z[d]) for d in range(3)
        ])

    def base(o):
        half = tensor if o == 0 else 1 - tensor
        return half * 512 + core * 256

    def gather_z(o, copies):
        wait_recv_all(copies)
        total = acc_x[o, rows_at(z * 16, 16), :]
        for d in range(3):
            total += got_z[o, d].astype(jnp.float32)
        mine = rows_at(base(o) + x * 64 + z * 16, 16)
        g[mine, :] = (total * scale).astype(jnp.bfloat16)
        return launch([remote(g.at[mine], g.at[mine], sends, recvs, 16 + o * 3 + d, peers_z[d]) for d in range(3)])

    def gather_x(o, copies):
        wait_recv_all(copies)
        mine = rows_at(base(o) + x * 64, 64)
        return launch([remote(g.at[mine], g.at[mine], sends, recvs, 22 + o * 3 + d, peers_x[d]) for d in range(3)])

    def gather_c(o, copies):
        wait_recv_all(copies)
        mine = rows_at(base(o), 256)
        return launch([remote(g.at[mine], g.at[mine], sends, recvs, 28 + o, partner)])

    arrive(1)
    c0 = multiply(0, act)
    x0 = reduce_x(0, c0)
    z0 = reduce_z(0, x0)
    wait_recv_all(fac_c)
    mine_z = rows_at(chip, 64)
    fac_z = launch([remote(fac.at[mine_z], fac.at[mine_z], sends, recvs, 30 + d, peers_z[d]) for d in range(3)])
    wait_recv_all(swap)
    c1 = multiply(1, act2)
    gz0 = gather_z(0, z0)
    x1 = reduce_x(1, c1)
    wait_recv_all(fac_z)
    mine_x = rows_at(x * 256, 256)
    fac_x = launch([remote(fac.at[mine_x], fac.at[mine_x], sends, recvs, 33 + d, peers_x[d]) for d in range(3)])
    gx0 = gather_x(0, gz0)
    z1 = reduce_z(1, x1)
    gz1 = gather_z(1, z1)
    gx1 = gather_x(1, gz1)
    gc0 = gather_c(0, gx0)
    gc1 = gather_c(1, gx1)
    wait_recv_all(gc0)
    wait_recv_all(gc1)

    arrive(6)
    arrive(7)
    turned[...] = lb[:, pl.ds(pl.multiple_of(fsdp // 4 * 128, 128), 128)].T
    half = nn(turned[rows_at(fsdp % 4 * 32, 32), :], g[...]).astype(bf)
    rotated = nn(half, rb[...])
    arrive(4)
    arrive(5)
    first = BETA_ONE * mom[...] + (1.0 - BETA_ONE) * rotated
    second = BETA_TWO * msq[...] + (1.0 - BETA_TWO) * rotated * rotated
    msq_out[...] = second
    normed = (first / (jnp.sqrt(second) + ADAM_EPS)).astype(bf)
    first = first.astype(bf)

    @pl.when(core == 0)
    def _():
        seen[rows_at(chip, 32), :] = normed
        out32[...] = first
        gm[...] = g[...]
        bo[...] = lb[...]

    @pl.when(core == 1)
    def _():
        seen[rows_at(chip + 32, 32), :] = first
        out32[...] = normed
        gm[...] = g[...].T
        bo[...] = rb[...]

    seen_c = launch([remote(out32, seen.at[rows_at(chip + core * 32, 32)], sends, recvs, 40, partner)])

    def square_rows(i, c):
        ff[tile(i), :] = nt(gm[tile(i), :], gm[...]) * ((1.0 - FACTOR_BETA) / N)
        return c

    lax.fori_loop(0, 4, square_rows, 0)
    wait_recv_all(seen_c)
    mine = rows_at(chip, 64)
    seen_z = launch([remote(seen.at[mine], seen.at[mine], sends, recvs, 41 + d, peers_z[d]) for d in range(3)])
    away = rows_at(chip + (1 - core) * 32, 32)
    kept_c = launch([remote(ff.at[away], kept, sends, recvs, 45, partner)])

    wait_recv_all(fac_x)
    for i in range(8):
        for k in range(5):
            j = (i + k) % 8
            block = fac[i * 128:(i + 1) * 128, k * 128:(k + 1) * 128]
            whole[i * 128:(i + 1) * 128, j * 128:(j + 1) * 128] = block
            if 0 < k < 4:
                whole[j * 128:(j + 1) * 128, i * 128:(i + 1) * 128] = block.T

    def power_rows(i, c):
        nxt = (FACTOR_BETA * whole[tile(i), :].astype(f32) + ff[tile(i), :]).astype(bf)
        p_ref[tile(i), :] = nn(nxt, bo[...]).astype(bf)
        return c

    lax.fori_loop(0, 4, power_rows, 0)
    p_copy = pltpu.make_async_copy(p_ref, p_own, local.at[11])
    p_copy.start()
    p_swap = launch([remote(p_ref, p_other, sends, recvs, 44, partner)])

    pt[...] = p_ref[...].T
    s_ref[...] = nt(pt[f, :], pt[f, :])
    a21[...] = nt(pt[h, :], pt[f, :])
    r1 = leaf(s_ref, x_ref, sh, sl, xh, xl)

    wait_recv_all(seen_z)
    mine = rows_at(x * 256, 256)
    seen_x = launch([remote(seen.at[mine], seen.at[mine], sends, recvs, 46 + d, peers_x[d]) for d in range(3)])

    def by_x(t):
        ta = tuple(v[:, a] for v in t)
        xa, x2 = (xh[a, a], xl[a, a]), (xh[b, :], xl[b, :])
        if len(t) == 1:
            return nt(ta[0], xa[0]) + nt(ta[0], xa[1]), nt(t[0], x2[0]) + nt(t[0], x2[1])
        return nt3(ta, xa), nt3(t, x2)

    def l_rows(i, c):
        u, v = by_x(split(a21[tile(i), :]))
        l21h[tile(i), a], l21l[tile(i), a] = split(u)
        l21h[tile(i), b], l21l[tile(i), b] = split(v)
        return c

    lax.fori_loop(0, 2, l_rows, 0)
    s_ref[...] = nt(pt[h, :], pt[h, :]) - nt3((l21h[...], l21l[...]), (l21h[...], l21l[...]))

    def q1_rows(i, c):
        u, v = by_x((p_ref[tile(i), f],))
        q_ref[tile(i), a], pt[tile(i), a] = split(u)
        q_ref[tile(i), b], pt[tile(i), b] = split(v)
        return c

    lax.fori_loop(0, 4, q1_rows, 0)
    first_half, last_half = pl.ds(0, H), pl.ds(H, H)
    q1_copy = pltpu.make_async_copy(q_ref.at[:, first_half], mine_out.at[:, first_half], local.at[13])
    q1_copy.start()
    q1_swap = launch([remote(q_ref.at[:, first_half], got_out.at[:, first_half], sends, recvs, 49, partner)])

    wait_recv_all(kept_c)
    ours, theirs = ff[rows_at(chip + core * 32, 32), :], kept[...]
    left_next[...] = FACTOR_BETA * lf[...] + jnp.where(core == 0, ours, theirs)
    right_next[...] = FACTOR_BETA * rf[...] + jnp.where(core == 0, theirs, ours)

    r2 = leaf(s_ref, x_ref, sh, sl, xh, xl)
    res_own[...] = jnp.full((8, 128), jnp.maximum(r1, r2), f32)
    res_c = launch([remote(res_own, res_got, sends, recvs, 50, partner)])

    wait_recv_all(seen_x)
    upd_c = remote(upd.at[pl.ds(32, 32)], upd.at[pl.ds(32, 32)], sends, recvs, 51, partner)
    first_copy = pltpu.make_async_copy(seen, first_all, local.at[12])
    first_c = remote(seen, first_all, sends, recvs, 52, partner)

    @pl.when(core == 0)
    def _():
        back = nn(lb[rows_at(chip, 64), :], seen[...]).astype(bf)
        upd[...] = nt(back, rb[...])
        upd_c.start()

    @pl.when(core == 1)
    def _():
        first_copy.start()
        first_c.start()

    def q2_rows(i, c):
        t = p_ref[tile(i), h].astype(f32) - nt3((q_ref[tile(i), f], pt[tile(i), f]), (l21h[...], l21l[...]))
        u, v = by_x(split(t))
        q_ref[tile(i), H:H + Q4] = u.astype(bf)
        q_ref[tile(i), H + Q4:N] = v.astype(bf)
        return c

    lax.fori_loop(0, 4, q2_rows, 0)
    q2_copy = pltpu.make_async_copy(q_ref.at[:, last_half], mine_out.at[:, last_half], local.at[14])
    q2_copy.start()
    q2_swap = launch([remote(q_ref.at[:, last_half], got_out.at[:, last_half], sends, recvs, 53, partner)])

    @pl.when(core == 1)
    def _():
        upd_c.wait_recv()

    arrive(8)
    arrive(9)
    delta = anc[...] - (par[...] - INNER_RATE * upd[rows_at(core * 32, 32), :])
    isl[island] = delta
    isl_y = launch([remote(isl.at[island], isl.at[island], sends, recvs, 54 + d, peers_y[d]) for d in range(3)])


    wait_recv_all(isl_y)
    average = (isl[0] + isl[1] + isl[2] + isl[3]) / 4.0
    arrive(10)
    momentum = OUTER_MOMENT * om[...] + average
    momentum_out[...] = momentum
    anchor_out[...] = anc[...] - OUTER_RATE * (average + OUTER_MOMENT * momentum)
    wait_recv_all(res_c)
    res_out[...] = jnp.maximum(res_own[...], res_got[...])
    wait_recv_all(p_swap)
    wait_recv_all(q1_swap)
    wait_recv_all(q2_swap)
    p_copy.wait()
    q1_copy.wait()
    q2_copy.wait()

    @pl.when(core == 0)
    def _():
        first_c.wait_recv()
        upd_c.wait_send()

    @pl.when(core == 1)
    def _():
        first_copy.wait()
        first_c.wait_send()

    for copy in started:
        copy.wait_send()


def step(scale, operands):
    bf, f32 = jnp.bfloat16, jnp.float32
    vm, hbm = pl.BlockSpec(memory_space=pltpu.VMEM), pl.BlockSpec(memory_space=pl.ANY)
    square = jax.ShapeDtypeStruct((N, N), bf)
    strip = jax.ShapeDtypeStruct((32, N), f32)
    big = pltpu.VMEM((N, N), bf)
    thin = pltpu.VMEM((32, N), f32)
    return pl.pallas_call(
        functools.partial(step_body, scale),
        out_shape=(square,) * 5 + (strip,) * 5 + (jax.ShapeDtypeStruct((8, 128), f32),),
        in_specs=[hbm] * 11,
        out_specs=(hbm,) * 5 + (vm,) * 6,
        scratch_shapes=[
            pltpu.VMEM((512, 512), bf), pltpu.VMEM((512, N), bf), thin, thin, thin, thin, big, big, thin, thin, thin,
            big,
            pltpu.VMEM((N, WIDE), bf),
            pltpu.VMEM((512, 512), bf),
            pltpu.VMEM((512, 512), bf),
            pltpu.VMEM((2, 256, N), f32),
            pltpu.VMEM((2, 256, N), bf),
            pltpu.VMEM((2, 256, N), bf),
            pltpu.VMEM((2, 3, 64, N), bf),
            pltpu.VMEM((2, 3, 64, N), bf),
            pltpu.VMEM((2, 64, N), f32),
            pltpu.VMEM((2, 3, 16, N), bf),
            pltpu.VMEM((2, 3, 16, N), bf),
            pltpu.VMEM((32, WIDE), bf),
            pltpu.VMEM((32, 2 * N), bf),
            pltpu.VMEM((128, N), bf),
            big,
            pltpu.VMEM((32, N), bf),
            big, big, big,
            pltpu.VMEM((N, N), f32),
            big, big, big,
            thin,
            pltpu.VMEM((64, N), f32),
            pltpu.VMEM((4, 32, N), f32),
            pltpu.VMEM((8, 128), f32),
            pltpu.VMEM((8, 128), f32),
            pltpu.VMEM((H, H), f32), pltpu.VMEM((H, H), f32), pltpu.VMEM((H, H), f32),
        ] + [pltpu.VMEM((H, H), bf)] * 6 + [
            pltpu.SemaphoreType.DMA((57,)),
            pltpu.SemaphoreType.DMA((57,)),
            pltpu.SemaphoreType.DMA((15,)),
        ],
        compiler_params=pltpu.CompilerParams(
            collective_id=0, has_side_effects=True, vmem_limit_bytes=VMEM_LIMIT
        ),
        name="step",
    )(*operands)


def orth_columns(power, gram, work, flip, out):
    flip[...] = power[...].T

    def fill(i, c):
        rows = rows_at(i * 128, 128)
        gram[rows, :] = nt(flip[rows, :], flip[...])
        work[rows, :] = power[rows, :].astype(jnp.float32)
        return c

    lax.fori_loop(0, 8, fill, 0)
    lane = lax.broadcasted_iota(jnp.int32, (1, N), 1)

    def column(k, c):
        row = gram[pl.ds(k, 1), :]
        at = lane == k
        scale = 1.0 / jnp.sqrt(jnp.sum(jnp.where(at, row, 0.0), 1, keepdims=True))
        upper = jnp.where(lane >= k, row * scale, 0.0)
        after = jnp.where(at, 0.0, upper)

        def strip(i, c):
            rows = rows_at(i * 128, 128)
            old = gram[rows, :]
            gram[rows, :] = old - jnp.sum(jnp.where(at, old, 0.0), 1, keepdims=True) * scale * upper
            old = work[rows, :]
            done = jnp.sum(jnp.where(at, old, 0.0), 1, keepdims=True) * scale
            work[rows, :] = jnp.where(at, done, old - done * after)
            return c

        return lax.fori_loop(0, 8, strip, c)

    lax.fori_loop(0, N, column, 0)
    out[...] = work[...].astype(jnp.bfloat16)


def finish_body(
    p_own, p_other, mine, got, first_in, lb_in, rb_in, msq, left_next, right_next, anchor, momentum, res_in,
    anchor_out, momentum_out, moment_out, msq_out, lnext_out, rnext_out, left_out, right_out,
    lb, rb, first, left_v, right_v, rows, res, turned, mrows, gram, work, power, flip, local,
):
    fsdp = lax.axis_index("fsdp")
    core = fsdp % 2
    load_res, load_l, load_f, load_r = [
        pltpu.make_async_copy(src, dst, local.at[i])
        for i, (src, dst) in enumerate(((res_in, res), (lb_in, lb), (first_in, first), (rb_in, rb)))
    ]
    start_all([load_res, load_l])

    def twice(v, mm, m):
        both = mm(jnp.concatenate(split(v), 0), m[...])
        return both[:32] + both[32:]

    passed = [
        (
            pltpu.make_async_copy(src, rows.at[i], local.at[6 + i]),
            pltpu.make_async_copy(rows.at[i], dst, local.at[6 + i]),
        )
        for i, (src, dst) in enumerate((
            (anchor, anchor_out), (momentum, momentum_out), (msq, msq_out), (left_next, lnext_out), (right_next, rnext_out),
        ))
    ]
    for copy_in, _ in passed:
        copy_in.start()

    def close(left, right):
        outs = [
            pltpu.make_async_copy(left, left_out, local.at[11]),
            pltpu.make_async_copy(right, right_out, local.at[12]),
        ]
        start_all(outs)
        columns = pl.ds(pl.multiple_of(fsdp // 4 * 128, 128), 128)
        turned[...] = left[:, columns].T
        turn = nn(turned[rows_at(fsdp % 4 * 32, 32), :], lb[...])
        load_f.wait()
        part = twice(turn, nn, first)
        load_r.wait()
        part = twice(part, nt, rb)
        mrows[...] = twice(part, nn, right)
        last = pltpu.make_async_copy(mrows, moment_out, local.at[13])
        last.start()
        for copy_in, copy_out in passed:
            copy_in.wait()
            copy_out.start()
        for _, copy_out in passed:
            copy_out.wait()
        for copy in outs + [last]:
            copy.wait()

    def fetch(left, right):
        load_left = pltpu.make_async_copy(left, left_v, local.at[4])
        load_right = pltpu.make_async_copy(right, right_v, local.at[5])
        start_all([load_left, load_f, load_r, load_right])
        load_l.wait()
        load_left.wait()
        load_right.wait()

    load_res.wait()
    good = jnp.sum(res[...]) < RESIDUAL_LIMIT * 1024.0

    @pl.when(jnp.logical_and(good, core == 0))
    def _():
        fetch(mine, got)

    @pl.when(jnp.logical_and(good, core == 1))
    def _():
        fetch(got, mine)

    @pl.when(jnp.logical_not(good))
    def _():
        def redo(side, out):
            @pl.when(core == side)
            def _():
                pltpu.sync_copy(p_own, power)

            @pl.when(core != side)
            def _():
                pltpu.sync_copy(p_other, power)

            orth_columns(power, gram, work, flip, out)

        start_all([load_f, load_r])
        load_l.wait()
        redo(0, left_v)
        redo(1, right_v)

    close(left_v, right_v)


def finish(operands):
    bf, f32 = jnp.bfloat16, jnp.float32
    hbm = pl.BlockSpec(memory_space=pl.ANY)
    square = jax.ShapeDtypeStruct((N, N), bf)
    strip = jax.ShapeDtypeStruct((32, N), f32)
    big = pltpu.VMEM((N, N), bf)
    return pl.pallas_call(
        finish_body,
        out_shape=(strip,) * 6 + (square,) * 2,
        in_specs=[hbm] * 13,
        out_specs=(hbm,) * 8,
        scratch_shapes=[
            big, big, big, big, big, pltpu.VMEM((5, 32, N), f32), pltpu.VMEM((8, 128), f32),
            pltpu.VMEM((128, N), bf), pltpu.VMEM((32, N), f32),
            pltpu.VMEM((N, N), f32), pltpu.VMEM((N, N), f32), big, big,
            pltpu.SemaphoreType.DMA((14,)),
        ],
        compiler_params=pltpu.CompilerParams(vmem_limit_bytes=FINISH_LIMIT),
        name="finish",
    )(*operands)


def per_device(
    activations,
    out_grads,
    moment,
    moment_sq,
    left_factor,
    right_factor,
    left_basis,
    right_basis,
    params,
    anchor,
    outer_momentum,
):
    scale = 1.0 / math.sqrt(activations.shape[1] * lax.axis_size("fsdp"))
    left_old, right_old = left_basis[0, 0], right_basis[0, 0]
    operands = (
        activations[0], out_grads[0], left_factor[0, 0], right_factor[0, 0], moment[0, 0], moment_sq[0, 0],
        left_old, right_old, params[0, 0], anchor[0], outer_momentum[0],
    )
    power, power_other, mine, got, first_all, *rows, residual = step(scale, operands)
    anchor_next, momentum_next, moment_next, second_moment, left_next, right_next, left_new, right_new = finish(
        (power, power_other, mine, got, first_all, left_old, right_old, *rows, residual)
    )
    return (
        anchor_next[None],
        momentum_next[None],
        moment_next[None, None],
        second_moment[None, None],
        left_next[None, None],
        right_next[None, None],
        left_new[None, None],
        right_new[None, None],
    )


def solution(mesh):
    in_specs = (
        P("island", "fsdp", "tensor"),
        P("island", "fsdp", "tensor"),
        P("island", "tensor", "fsdp", None),
        P("island", "tensor", "fsdp", None),
        P("island", "tensor", "fsdp", None),
        P("island", "tensor", "fsdp", None),
        P("island", "tensor", None, None),
        P("island", "tensor", None, None),
        P("island", "tensor", "fsdp", None),
        P("tensor", "fsdp", None),
        P("tensor", "fsdp", None),
    )
    out_specs = (
        P("tensor", "fsdp", None),
        P("tensor", "fsdp", None),
        P("island", "tensor", "fsdp", None),
        P("island", "tensor", "fsdp", None),
        P("island", "tensor", "fsdp", None),
        P("island", "tensor", "fsdp", None),
        P("island", "tensor", None, None),
        P("island", "tensor", None, None),
    )
    return jax.shard_map(
        per_device, mesh=mesh, in_specs=in_specs, out_specs=out_specs, check_vma=False
    )
```

```python
import functools
import math

import jax
import jax.numpy as jnp
from jax import lax
from jax.experimental import pallas as pl
from jax.experimental.pallas import tpu as pltpu
from jax.sharding import PartitionSpec as P

BETA_ONE = 0.9
BETA_TWO = 0.95
FACTOR_BETA = 0.9
ADAM_EPS = 1e-08
INNER_RATE = 0.5
OUTER_RATE = 0.7
OUTER_MOMENT = 0.9
RESIDUAL_LIMIT = 0.06

N = 1024
H = 512
Q4 = 256
ROUGH = 3
VMEM_LIMIT = 58 * 1024 * 1024
FINISH_LIMIT = 60 * 1024 * 1024


def nn(a, b):
    return jnp.dot(a, b, preferred_element_type=jnp.float32)


def nt(a, b):
    return lax.dot_general(a, b, (((1,), (1,)), ((), ())), preferred_element_type=jnp.float32)


def split(x):
    hi = x.astype(jnp.bfloat16)
    return hi, (x - hi.astype(jnp.float32)).astype(jnp.bfloat16)


def nt3(a, b):
    return nt(a[0], b[0]) + (nt(a[0], b[1]) + nt(a[1], b[0]))


def nn3(a, b):
    return nn(a[0], b[0]) + (nn(a[0], b[1]) + nn(a[1], b[0]))


def iotas(n):
    return lax.broadcasted_iota(jnp.int32, (n, n), 0), lax.broadcasted_iota(jnp.int32, (n, n), 1)


def low(e):
    r, c = iotas(e.shape[0])
    return jnp.where(r > c, e, jnp.where(r == c, 0.5 * e, 0.0))


def minus_eye(e):
    r, c = iotas(e.shape[0])
    return jnp.where(r == c, e - 1.0, e)


def diag_rows(s):
    r, c = iotas(s.shape[0])
    picked = jnp.where(r == c, s, 0.0)
    return jnp.sum(picked, 1, keepdims=True), jnp.sum(picked, 0, keepdims=True)


def residual(x, s, y_ref):
    a, b = slice(0, Q4), slice(Q4, H)
    if len(x) == 1:
        xa, x2 = x[0][a, a], x[0][b, :]
        ya = nn(xa, s[0][a, a]).astype(jnp.bfloat16)
        y2 = nn(x2, s[0][...]).astype(jnp.bfloat16)
        return nt(ya, xa), nt(y2[:, a], xa), nt(y2, x2)
    xa = (x[0][a, a], x[1][a, a])
    x2 = (x[0][b, :], x[1][b, :])
    ya = split(nn3(xa, (s[0][a, a], s[1][a, a])))
    y2 = split(nn3(x2, (s[0][...], s[1][...])))
    y2a = (y2[0][:, a], y2[1][:, a])
    return nt3(ya, xa), nt3(y2a, xa), nt3(y2, x2)


def leaf(s_ref, x_ref, sh, sl, xh, xl):
    a, b = slice(0, Q4), slice(Q4, H)
    dc, dr = diag_rows(s_ref[...])
    dc, dr = lax.rsqrt(dc), lax.rsqrt(dr)
    sn = s_ref[...] * dc * dr
    hi, lo = split(sn)
    sh[...] = hi
    sl[...] = lo
    e0 = minus_eye(sn)
    f0 = low(e0)
    r, c = iotas(H)
    x0 = jnp.where(r == c, 1.0 - f0, -f0)
    x_ref[...] = x0
    xh[...] = x0.astype(jnp.bfloat16)

    def update(e, fine):
        eaa, eca, edd = e
        faa, fdd = low(eaa).astype(jnp.bfloat16), low(edd).astype(jnp.bfloat16)
        fca = eca.astype(jnp.bfloat16)
        xa, xc, xd = xh[a, a], xh[b, a], xh[b, b]
        na = x_ref[a, a] - nn(faa, xa)
        nc = x_ref[b, a] - (nn(fca, xa) + nn(fdd, xc))
        nd = x_ref[b, b] - nn(fdd, xd)
        x_ref[a, a] = na
        x_ref[b, a] = nc
        x_ref[b, b] = nd
        if not fine:
            xh[a, a] = na.astype(jnp.bfloat16)
            xh[b, a] = nc.astype(jnp.bfloat16)
            xh[b, b] = nd.astype(jnp.bfloat16)

    def step(_, carry):
        eaa, eca, edd = residual((xh,), (sh,), None)
        update((minus_eye(eaa), eca, minus_eye(edd)), False)
        return carry

    lax.fori_loop(0, ROUGH, step, 0)
    hi, lo = split(x_ref[...])
    xh[...] = hi
    xl[...] = lo
    eaa, eca, edd = residual((xh, xl), (sh, sl), None)
    eaa, edd = minus_eye(eaa), minus_eye(edd)
    left = jnp.sum(eaa * eaa) + 2.0 * jnp.sum(eca * eca) + jnp.sum(edd * edd)
    update((eaa, eca, edd), True)
    x_ref[...] = x_ref[...] * dr
    hi, lo = split(x_ref[...])
    xh[...] = hi
    xl[...] = lo
    return left


WIDE = 640


MESH_ID = pl.DeviceIdType.MESH


def place():
    f = lax.axis_index("fsdp")
    return f // 8, (f // 2) % 4, f % 2


def to_device(x, z, core):
    return {"fsdp": (x * 4 + z) * 2 + core}


def greet(peers):
    barrier = pltpu.get_barrier_semaphore()
    for peer in peers:
        pl.semaphore_signal(barrier, inc=1, device_id=peer, device_id_type=MESH_ID)
    pl.semaphore_wait(barrier, len(peers))


def remote(src, dst, sends, recvs, index, peer):
    return pltpu.make_async_remote_copy(
        src_ref=src,
        dst_ref=dst,
        send_sem=sends.at[index],
        recv_sem=recvs.at[index],
        device_id=peer,
        device_id_type=MESH_ID,
    )


def rows_at(start, count):
    return pl.ds(pl.multiple_of(start, count), count)


def start_all(copies):
    for copy in copies:
        copy.start()


def wait_recv_all(copies):
    for copy in copies:
        copy.wait_recv()


def step_body(
    scale, act_in, grads_in, lf_in, rf_in, mom_in, msq_in, lb_in, rb_in, par_in, anc_in, om_in,
    p_own, p_other, mine_out, got_out, first_all,
    msq_out, left_next, right_next, anchor_out, momentum_out, res_out,
    act, grads, lf, rf, mom, msq, lb, rb, par, anc, om,
    g, fac, act2, flip, part, sent_c, got_c, sent_x, got_x, acc_x, sent_z, got_z, sent_f, twice,
    turned, seen, out32, whole, gm, bo, ff, p_ref, pt, q_ref, kept, upd, isl, res_own, res_got,
    s_ref, a21, x_ref, sh, sl, xh, xl, l21h, l21l, sends, recvs, local,
):
    bf, f32 = jnp.bfloat16, jnp.float32
    pairs = (
        (act_in, act), (grads_in, grads), (lf_in, lf), (rf_in, rf), (mom_in, mom), (msq_in, msq),
        (lb_in, lb), (rb_in, rb), (par_in, par), (anc_in, anc), (om_in, om),
    )
    loads = [pltpu.make_async_copy(src, dst, local.at[i]) for i, (src, dst) in enumerate(pairs)]
    start_all(loads)

    def arrive(i):
        loads[i].wait()

    fsdp, island, tensor = lax.axis_index("fsdp"), lax.axis_index("island"), lax.axis_index("tensor")
    x, z, core = place()
    partner = to_device(x, z, 1 - core)
    peers_x = [to_device((x + d) % 4, z, core) for d in (1, 2, 3)]
    peers_z = [to_device(x, (z + d) % 4, core) for d in (1, 2, 3)]
    peers_y = [{"island": (island + d) % 4} for d in (1, 2, 3)]
    other = {"tensor": 1 - tensor}
    chip = (x * 4 + z) * 64
    f, h = slice(0, H), slice(H, N)
    a, b = slice(0, Q4), slice(Q4, H)
    greet([partner, other] + peers_x + peers_z + peers_y)
    started = []

    def launch(copies):
        start_all(copies)
        started.extend(copies)
        return copies

    def tile(i):
        return rows_at(i * Q4, Q4)

    arrive(0)
    swap = launch([remote(act, act2, sends, recvs, 0, other)])

    arrive(2)
    arrive(3)
    near = pl.ds(pl.multiple_of(chip // 128 * 128, 128), WIDE)

    def pack(factor):
        narrow = factor[...].astype(jnp.bfloat16)
        twice[:, :N] = narrow
        twice[:, N:] = narrow
        return twice[:, near]

    @pl.when(core == 0)
    def _():
        fac[rows_at(chip, 32), :] = pack(lf)
        sent_f[...] = pack(rf)

    @pl.when(core == 1)
    def _():
        fac[rows_at(chip + 32, 32), :] = pack(rf)
        sent_f[...] = pack(lf)

    fac_c = launch([remote(sent_f, fac.at[rows_at(chip + core * 32, 32)], sends, recvs, 1, partner)])

    def multiply(o, source):
        flip[...] = source[...].T
        sent_c[o] = nn(flip[rows_at((1 - core) * 256, 256), :], grads[...]).astype(jnp.bfloat16)
        copies = launch([remote(sent_c.at[o], got_c.at[o], sends, recvs, 2 + o, partner)])
        part[o] = nn(flip[rows_at(core * 256, 256), :], grads[...])
        return copies

    def reduce_x(o, copies):
        wait_recv_all(copies)
        part[o] += got_c[o].astype(jnp.float32)
        for d in (1, 2, 3):
            sent_x[o, d - 1] = part[o, rows_at((x + d) % 4 * 64, 64), :].astype(jnp.bfloat16)
        return launch([
            remote(sent_x.at[o, d], got_x.at[o, d], sends, recvs, 4 + o * 3 + d, peers_x[d]) for d in range(3)
        ])

    def reduce_z(o, copies):
        wait_recv_all(copies)
        total = part[o, rows_at(x * 64, 64), :]
        for d in range(3):
            total += got_x[o, d].astype(jnp.float32)
        acc_x[o] = total
        for d in (1, 2, 3):
            sent_z[o, d - 1] = acc_x[o, rows_at((z + d) % 4 * 16, 16), :].astype(jnp.bfloat16)
        return launch([
            remote(sent_z.at[o, d], got_z.at[o, d], sends, recvs, 10 + o * 3 + d, peers_z[d]) for d in range(3)
        ])

    def base(o):
        half = tensor if o == 0 else 1 - tensor
        return half * 512 + core * 256

    def gather_z(o, copies):
        wait_recv_all(copies)
        total = acc_x[o, rows_at(z * 16, 16), :]
        for d in range(3):
            total += got_z[o, d].astype(jnp.float32)
        mine = rows_at(base(o) + x * 64 + z * 16, 16)
        g[mine, :] = (total * scale).astype(jnp.bfloat16)
        return launch([remote(g.at[mine], g.at[mine], sends, recvs, 16 + o * 3 + d, peers_z[d]) for d in range(3)])

    def gather_x(o, copies):
        wait_recv_all(copies)
        mine = rows_at(base(o) + x * 64, 64)
        return launch([remote(g.at[mine], g.at[mine], sends, recvs, 22 + o * 3 + d, peers_x[d]) for d in range(3)])

    def gather_c(o, copies):
        wait_recv_all(copies)
        mine = rows_at(base(o), 256)
        return launch([remote(g.at[mine], g.at[mine], sends, recvs, 28 + o, partner)])

    arrive(1)
    c0 = multiply(0, act)
    x0 = reduce_x(0, c0)
    z0 = reduce_z(0, x0)
    wait_recv_all(swap)
    c1 = multiply(1, act2)
    wait_recv_all(fac_c)
    mine_z = rows_at(chip, 64)
    fac_z = launch([remote(fac.at[mine_z], fac.at[mine_z], sends, recvs, 30 + d, peers_z[d]) for d in range(3)])
    gz0 = gather_z(0, z0)
    x1 = reduce_x(1, c1)
    gx0 = gather_x(0, gz0)
    z1 = reduce_z(1, x1)
    gz1 = gather_z(1, z1)
    gx1 = gather_x(1, gz1)
    wait_recv_all(fac_z)
    mine_x = rows_at(x * 256, 256)
    fac_x = launch([remote(fac.at[mine_x], fac.at[mine_x], sends, recvs, 33 + d, peers_x[d]) for d in range(3)])
    gc0 = gather_c(0, gx0)
    gc1 = gather_c(1, gx1)
    wait_recv_all(gc0)
    wait_recv_all(gc1)

    arrive(6)
    arrive(7)
    turned[...] = lb[:, pl.ds(pl.multiple_of(fsdp // 4 * 128, 128), 128)].T
    half = nn(turned[rows_at(fsdp % 4 * 32, 32), :], g[...]).astype(bf)
    rotated = nn(half, rb[...])
    arrive(4)
    arrive(5)
    first = BETA_ONE * mom[...] + (1.0 - BETA_ONE) * rotated
    second = BETA_TWO * msq[...] + (1.0 - BETA_TWO) * rotated * rotated
    msq_out[...] = second
    normed = (first / (jnp.sqrt(second) + ADAM_EPS)).astype(bf)
    first = first.astype(bf)

    @pl.when(core == 0)
    def _():
        seen[rows_at(chip, 32), :] = normed
        out32[...] = first
        gm[...] = g[...]
        bo[...] = lb[...]

    @pl.when(core == 1)
    def _():
        seen[rows_at(chip + 32, 32), :] = first
        out32[...] = normed
        gm[...] = g[...].T
        bo[...] = rb[...]

    seen_c = launch([remote(out32, seen.at[rows_at(chip + core * 32, 32)], sends, recvs, 40, partner)])

    def square_rows(i, c):
        ff[tile(i), :] = nt(gm[tile(i), :], gm[...]) * ((1.0 - FACTOR_BETA) / N)
        return c

    lax.fori_loop(0, 4, square_rows, 0)
    wait_recv_all(seen_c)
    mine = rows_at(chip, 64)
    seen_z = launch([remote(seen.at[mine], seen.at[mine], sends, recvs, 41 + d, peers_z[d]) for d in range(3)])
    away = rows_at(chip + (1 - core) * 32, 32)
    kept_c = launch([remote(ff.at[away], kept, sends, recvs, 45, partner)])

    wait_recv_all(fac_x)
    for i in range(8):
        for k in range(5):
            j = (i + k) % 8
            block = fac[i * 128:(i + 1) * 128, k * 128:(k + 1) * 128]
            whole[i * 128:(i + 1) * 128, j * 128:(j + 1) * 128] = block
            if 0 < k < 4:
                whole[j * 128:(j + 1) * 128, i * 128:(i + 1) * 128] = block.T

    def power_rows(i, c):
        nxt = (FACTOR_BETA * whole[tile(i), :].astype(f32) + ff[tile(i), :]).astype(bf)
        p_ref[tile(i), :] = nn(nxt, bo[...]).astype(bf)
        return c

    lax.fori_loop(0, 4, power_rows, 0)
    p_copy = pltpu.make_async_copy(p_ref, p_own, local.at[11])
    p_copy.start()
    p_swap = launch([remote(p_ref, p_other, sends, recvs, 44, partner)])

    pt[...] = p_ref[...].T
    s_ref[...] = nt(pt[f, :], pt[f, :])
    a21[...] = nt(pt[h, :], pt[f, :])
    r1 = leaf(s_ref, x_ref, sh, sl, xh, xl)

    wait_recv_all(seen_z)
    mine = rows_at(x * 256, 256)
    seen_x = launch([remote(seen.at[mine], seen.at[mine], sends, recvs, 46 + d, peers_x[d]) for d in range(3)])

    def by_x(t):
        ta = tuple(v[:, a] for v in t)
        xa, x2 = (xh[a, a], xl[a, a]), (xh[b, :], xl[b, :])
        if len(t) == 1:
            return nt(ta[0], xa[0]) + nt(ta[0], xa[1]), nt(t[0], x2[0]) + nt(t[0], x2[1])
        return nt3(ta, xa), nt3(t, x2)

    def l_rows(i, c):
        u, v = by_x(split(a21[tile(i), :]))
        l21h[tile(i), a], l21l[tile(i), a] = split(u)
        l21h[tile(i), b], l21l[tile(i), b] = split(v)
        return c

    lax.fori_loop(0, 2, l_rows, 0)
    s_ref[...] = nt(pt[h, :], pt[h, :]) - nt3((l21h[...], l21l[...]), (l21h[...], l21l[...]))

    def q1_rows(i, c):
        u, v = by_x((p_ref[tile(i), f],))
        q_ref[tile(i), a], pt[tile(i), a] = split(u)
        q_ref[tile(i), b], pt[tile(i), b] = split(v)
        return c

    lax.fori_loop(0, 4, q1_rows, 0)
    first_half, last_half = pl.ds(0, H), pl.ds(H, H)
    q1_copy = pltpu.make_async_copy(q_ref.at[:, first_half], mine_out.at[:, first_half], local.at[13])
    q1_copy.start()
    q1_swap = launch([remote(q_ref.at[:, first_half], got_out.at[:, first_half], sends, recvs, 49, partner)])

    wait_recv_all(kept_c)
    ours, theirs = ff[rows_at(chip + core * 32, 32), :], kept[...]
    left_next[...] = FACTOR_BETA * lf[...] + jnp.where(core == 0, ours, theirs)
    right_next[...] = FACTOR_BETA * rf[...] + jnp.where(core == 0, theirs, ours)

    r2 = leaf(s_ref, x_ref, sh, sl, xh, xl)
    res_own[...] = jnp.full((8, 128), jnp.maximum(r1, r2), f32)
    res_c = launch([remote(res_own, res_got, sends, recvs, 50, partner)])

    wait_recv_all(seen_x)
    upd_c = remote(upd.at[pl.ds(32, 32)], upd.at[pl.ds(32, 32)], sends, recvs, 51, partner)
    first_copy = pltpu.make_async_copy(seen, first_all, local.at[12])
    first_c = remote(seen, first_all, sends, recvs, 52, partner)

    @pl.when(core == 0)
    def _():
        back = nn(lb[rows_at(chip, 64), :], seen[...]).astype(bf)
        upd[...] = nt(back, rb[...])
        upd_c.start()

    @pl.when(core == 1)
    def _():
        first_copy.start()
        first_c.start()

    def q2_rows(i, c):
        t = p_ref[tile(i), h].astype(f32) - nt3((q_ref[tile(i), f], pt[tile(i), f]), (l21h[...], l21l[...]))
        u, v = by_x(split(t))
        q_ref[tile(i), H:H + Q4] = u.astype(bf)
        q_ref[tile(i), H + Q4:N] = v.astype(bf)
        return c

    lax.fori_loop(0, 4, q2_rows, 0)
    q2_copy = pltpu.make_async_copy(q_ref.at[:, last_half], mine_out.at[:, last_half], local.at[14])
    q2_copy.start()
    q2_swap = launch([remote(q_ref.at[:, last_half], got_out.at[:, last_half], sends, recvs, 53, partner)])

    @pl.when(core == 1)
    def _():
        upd_c.wait_recv()

    arrive(8)
    arrive(9)
    delta = anc[...] - (par[...] - INNER_RATE * upd[rows_at(core * 32, 32), :])
    isl[island] = delta
    isl_y = launch([remote(isl.at[island], isl.at[island], sends, recvs, 54 + d, peers_y[d]) for d in range(3)])


    wait_recv_all(isl_y)
    average = (isl[0] + isl[1] + isl[2] + isl[3]) / 4.0
    arrive(10)
    momentum = OUTER_MOMENT * om[...] + average
    momentum_out[...] = momentum
    anchor_out[...] = anc[...] - OUTER_RATE * (average + OUTER_MOMENT * momentum)
    wait_recv_all(res_c)
    res_out[...] = jnp.maximum(res_own[...], res_got[...])
    wait_recv_all(p_swap)
    wait_recv_all(q1_swap)
    wait_recv_all(q2_swap)
    p_copy.wait()
    q1_copy.wait()
    q2_copy.wait()

    @pl.when(core == 0)
    def _():
        first_c.wait_recv()
        upd_c.wait_send()

    @pl.when(core == 1)
    def _():
        first_copy.wait()
        first_c.wait_send()

    for copy in started:
        copy.wait_send()


def step(scale, operands):
    bf, f32 = jnp.bfloat16, jnp.float32
    vm, hbm = pl.BlockSpec(memory_space=pltpu.VMEM), pl.BlockSpec(memory_space=pl.ANY)
    square = jax.ShapeDtypeStruct((N, N), bf)
    strip = jax.ShapeDtypeStruct((32, N), f32)
    big = pltpu.VMEM((N, N), bf)
    thin = pltpu.VMEM((32, N), f32)
    return pl.pallas_call(
        functools.partial(step_body, scale),
        out_shape=(square,) * 5 + (strip,) * 5 + (jax.ShapeDtypeStruct((8, 128), f32),),
        in_specs=[hbm] * 11,
        out_specs=(hbm,) * 5 + (vm,) * 6,
        scratch_shapes=[
            pltpu.VMEM((512, 512), bf), pltpu.VMEM((512, N), bf), thin, thin, thin, thin, big, big, thin, thin, thin,
            big,
            pltpu.VMEM((N, WIDE), bf),
            pltpu.VMEM((512, 512), bf),
            pltpu.VMEM((512, 512), bf),
            pltpu.VMEM((2, 256, N), f32),
            pltpu.VMEM((2, 256, N), bf),
            pltpu.VMEM((2, 256, N), bf),
            pltpu.VMEM((2, 3, 64, N), bf),
            pltpu.VMEM((2, 3, 64, N), bf),
            pltpu.VMEM((2, 64, N), f32),
            pltpu.VMEM((2, 3, 16, N), bf),
            pltpu.VMEM((2, 3, 16, N), bf),
            pltpu.VMEM((32, WIDE), bf),
            pltpu.VMEM((32, 2 * N), bf),
            pltpu.VMEM((128, N), bf),
            big,
            pltpu.VMEM((32, N), bf),
            big, big, big,
            pltpu.VMEM((N, N), f32),
            big, big, big,
            thin,
            pltpu.VMEM((64, N), f32),
            pltpu.VMEM((4, 32, N), f32),
            pltpu.VMEM((8, 128), f32),
            pltpu.VMEM((8, 128), f32),
            pltpu.VMEM((H, H), f32), pltpu.VMEM((H, H), f32), pltpu.VMEM((H, H), f32),
        ] + [pltpu.VMEM((H, H), bf)] * 6 + [
            pltpu.SemaphoreType.DMA((57,)),
            pltpu.SemaphoreType.DMA((57,)),
            pltpu.SemaphoreType.DMA((15,)),
        ],
        compiler_params=pltpu.CompilerParams(
            collective_id=0, has_side_effects=True, vmem_limit_bytes=VMEM_LIMIT
        ),
        name="step",
    )(*operands)


def orth_columns(power, gram, work, flip, out):
    flip[...] = power[...].T

    def fill(i, c):
        rows = rows_at(i * 128, 128)
        gram[rows, :] = nt(flip[rows, :], flip[...])
        work[rows, :] = power[rows, :].astype(jnp.float32)
        return c

    lax.fori_loop(0, 8, fill, 0)
    lane = lax.broadcasted_iota(jnp.int32, (1, N), 1)

    def column(k, c):
        row = gram[pl.ds(k, 1), :]
        at = lane == k
        scale = 1.0 / jnp.sqrt(jnp.sum(jnp.where(at, row, 0.0), 1, keepdims=True))
        upper = jnp.where(lane >= k, row * scale, 0.0)
        after = jnp.where(at, 0.0, upper)

        def strip(i, c):
            rows = rows_at(i * 128, 128)
            old = gram[rows, :]
            gram[rows, :] = old - jnp.sum(jnp.where(at, old, 0.0), 1, keepdims=True) * scale * upper
            old = work[rows, :]
            done = jnp.sum(jnp.where(at, old, 0.0), 1, keepdims=True) * scale
            work[rows, :] = jnp.where(at, done, old - done * after)
            return c

        return lax.fori_loop(0, 8, strip, c)

    lax.fori_loop(0, N, column, 0)
    out[...] = work[...].astype(jnp.bfloat16)


def finish_body(
    p_own, p_other, mine, got, first_in, lb_in, rb_in, msq, left_next, right_next, anchor, momentum, res_in,
    anchor_out, momentum_out, moment_out, msq_out, lnext_out, rnext_out, left_out, right_out,
    lb, rb, first, left_v, right_v, rows, res, turned, mrows, gram, work, power, flip, local,
):
    fsdp = lax.axis_index("fsdp")
    core = fsdp % 2
    load_res, load_l, load_f, load_r = [
        pltpu.make_async_copy(src, dst, local.at[i])
        for i, (src, dst) in enumerate(((res_in, res), (lb_in, lb), (first_in, first), (rb_in, rb)))
    ]
    start_all([load_res, load_l])

    def twice(v, mm, m):
        both = mm(jnp.concatenate(split(v), 0), m[...])
        return both[:32] + both[32:]

    passed = [
        (
            pltpu.make_async_copy(src, rows.at[i], local.at[6 + i]),
            pltpu.make_async_copy(rows.at[i], dst, local.at[6 + i]),
        )
        for i, (src, dst) in enumerate((
            (anchor, anchor_out), (momentum, momentum_out), (msq, msq_out), (left_next, lnext_out), (right_next, rnext_out),
        ))
    ]
    for copy_in, _ in passed:
        copy_in.start()

    def close(left, right):
        outs = [
            pltpu.make_async_copy(left, left_out, local.at[11]),
            pltpu.make_async_copy(right, right_out, local.at[12]),
        ]
        start_all(outs)
        columns = pl.ds(pl.multiple_of(fsdp // 4 * 128, 128), 128)
        turned[...] = left[:, columns].T
        turn = nn(turned[rows_at(fsdp % 4 * 32, 32), :], lb[...])
        load_f.wait()
        part = twice(turn, nn, first)
        load_r.wait()
        part = twice(part, nt, rb)
        mrows[...] = twice(part, nn, right)
        last = pltpu.make_async_copy(mrows, moment_out, local.at[13])
        last.start()
        for copy_in, copy_out in passed:
            copy_in.wait()
            copy_out.start()
        for _, copy_out in passed:
            copy_out.wait()
        for copy in outs + [last]:
            copy.wait()

    def fetch(left, right):
        load_left = pltpu.make_async_copy(left, left_v, local.at[4])
        load_right = pltpu.make_async_copy(right, right_v, local.at[5])
        start_all([load_left, load_f, load_r, load_right])
        load_l.wait()
        load_left.wait()
        load_right.wait()

    load_res.wait()
    good = jnp.sum(res[...]) < RESIDUAL_LIMIT * 1024.0

    @pl.when(jnp.logical_and(good, core == 0))
    def _():
        fetch(mine, got)

    @pl.when(jnp.logical_and(good, core == 1))
    def _():
        fetch(got, mine)

    @pl.when(jnp.logical_not(good))
    def _():
        def redo(side, out):
            @pl.when(core == side)
            def _():
                pltpu.sync_copy(p_own, power)

            @pl.when(core != side)
            def _():
                pltpu.sync_copy(p_other, power)

            orth_columns(power, gram, work, flip, out)

        start_all([load_f, load_r])
        load_l.wait()
        redo(0, left_v)
        redo(1, right_v)

    close(left_v, right_v)


def finish(operands):
    bf, f32 = jnp.bfloat16, jnp.float32
    hbm = pl.BlockSpec(memory_space=pl.ANY)
    square = jax.ShapeDtypeStruct((N, N), bf)
    strip = jax.ShapeDtypeStruct((32, N), f32)
    big = pltpu.VMEM((N, N), bf)
    return pl.pallas_call(
        finish_body,
        out_shape=(strip,) * 6 + (square,) * 2,
        in_specs=[hbm] * 13,
        out_specs=(hbm,) * 8,
        scratch_shapes=[
            big, big, big, big, big, pltpu.VMEM((5, 32, N), f32), pltpu.VMEM((8, 128), f32),
            pltpu.VMEM((128, N), bf), pltpu.VMEM((32, N), f32),
            pltpu.VMEM((N, N), f32), pltpu.VMEM((N, N), f32), big, big,
            pltpu.SemaphoreType.DMA((14,)),
        ],
        compiler_params=pltpu.CompilerParams(vmem_limit_bytes=FINISH_LIMIT),
        name="finish",
    )(*operands)


def per_device(
    activations,
    out_grads,
    moment,
    moment_sq,
    left_factor,
    right_factor,
    left_basis,
    right_basis,
    params,
    anchor,
    outer_momentum,
):
    scale = 1.0 / math.sqrt(activations.shape[1] * lax.axis_size("fsdp"))
    left_old, right_old = left_basis[0, 0], right_basis[0, 0]
    operands = (
        activations[0], out_grads[0], left_factor[0, 0], right_factor[0, 0], moment[0, 0], moment_sq[0, 0],
        left_old, right_old, params[0, 0], anchor[0], outer_momentum[0],
    )
    power, power_other, mine, got, first_all, *rows, residual = step(scale, operands)
    anchor_next, momentum_next, moment_next, second_moment, left_next, right_next, left_new, right_new = finish(
        (power, power_other, mine, got, first_all, left_old, right_old, *rows, residual)
    )
    return (
        anchor_next[None],
        momentum_next[None],
        moment_next[None, None],
        second_moment[None, None],
        left_next[None, None],
        right_next[None, None],
        left_new[None, None],
        right_new[None, None],
    )


def solution(mesh):
    in_specs = (
        P("island", "fsdp", "tensor"),
        P("island", "fsdp", "tensor"),
        P("island", "tensor", "fsdp", None),
        P("island", "tensor", "fsdp", None),
        P("island", "tensor", "fsdp", None),
        P("island", "tensor", "fsdp", None),
        P("island", "tensor", None, None),
        P("island", "tensor", None, None),
        P("island", "tensor", "fsdp", None),
        P("tensor", "fsdp", None),
        P("tensor", "fsdp", None),
    )
    out_specs = (
        P("tensor", "fsdp", None),
        P("tensor", "fsdp", None),
        P("island", "tensor", "fsdp", None),
        P("island", "tensor", "fsdp", None),
        P("island", "tensor", "fsdp", None),
        P("island", "tensor", "fsdp", None),
        P("island", "tensor", None, None),
        P("island", "tensor", None, None),
    )
    return jax.shard_map(
        per_device, mesh=mesh, in_specs=in_specs, out_specs=out_specs, check_vma=False
    )
```

```python
import functools
import math

import jax
import jax.numpy as jnp
from jax import lax
from jax.experimental import pallas as pl
from jax.experimental.pallas import tpu as pltpu
from jax.sharding import PartitionSpec as P

BETA_ONE = 0.9
BETA_TWO = 0.95
FACTOR_BETA = 0.9
ADAM_EPS = 1e-08
INNER_RATE = 0.5
OUTER_RATE = 0.7
OUTER_MOMENT = 0.9
RESIDUAL_LIMIT = 0.06

N = 1024
H = 512
Q4 = 256
ROUGH = 3
VMEM_LIMIT = 58 * 1024 * 1024
FINISH_LIMIT = 60 * 1024 * 1024


def nn(a, b):
    return jnp.dot(a, b, preferred_element_type=jnp.float32)


def nt(a, b):
    return lax.dot_general(a, b, (((1,), (1,)), ((), ())), preferred_element_type=jnp.float32)


def split(x):
    hi = x.astype(jnp.bfloat16)
    return hi, (x - hi.astype(jnp.float32)).astype(jnp.bfloat16)


def nt3(a, b):
    return nt(a[0], b[0]) + (nt(a[0], b[1]) + nt(a[1], b[0]))


def nn3(a, b):
    return nn(a[0], b[0]) + (nn(a[0], b[1]) + nn(a[1], b[0]))


def iotas(n):
    return lax.broadcasted_iota(jnp.int32, (n, n), 0), lax.broadcasted_iota(jnp.int32, (n, n), 1)


def low(e):
    r, c = iotas(e.shape[0])
    return jnp.where(r > c, e, jnp.where(r == c, 0.5 * e, 0.0))


def minus_eye(e):
    r, c = iotas(e.shape[0])
    return jnp.where(r == c, e - 1.0, e)


def diag_rows(s):
    r, c = iotas(s.shape[0])
    picked = jnp.where(r == c, s, 0.0)
    return jnp.sum(picked, 1, keepdims=True), jnp.sum(picked, 0, keepdims=True)


def residual(x, s, y_ref):
    a, b = slice(0, Q4), slice(Q4, H)
    if len(x) == 1:
        xa, x2 = x[0][a, a], x[0][b, :]
        ya = nn(xa, s[0][a, a]).astype(jnp.bfloat16)
        y2 = nn(x2, s[0][...]).astype(jnp.bfloat16)
        return nt(ya, xa), nt(y2[:, a], xa), nt(y2, x2)
    xa = (x[0][a, a], x[1][a, a])
    x2 = (x[0][b, :], x[1][b, :])
    ya = split(nn3(xa, (s[0][a, a], s[1][a, a])))
    y2 = split(nn3(x2, (s[0][...], s[1][...])))
    y2a = (y2[0][:, a], y2[1][:, a])
    return nt3(ya, xa), nt3(y2a, xa), nt3(y2, x2)


def leaf(s_ref, x_ref, sh, sl, xh, xl):
    a, b = slice(0, Q4), slice(Q4, H)
    dc, dr = diag_rows(s_ref[...])
    dc, dr = lax.rsqrt(dc), lax.rsqrt(dr)
    sn = s_ref[...] * dc * dr
    hi, lo = split(sn)
    sh[...] = hi
    sl[...] = lo
    e0 = minus_eye(sn)
    f0 = low(e0)
    r, c = iotas(H)
    x0 = jnp.where(r == c, 1.0 - f0, -f0)
    x_ref[...] = x0
    xh[...] = x0.astype(jnp.bfloat16)

    def update(e, fine):
        eaa, eca, edd = e
        faa, fdd = low(eaa).astype(jnp.bfloat16), low(edd).astype(jnp.bfloat16)
        fca = eca.astype(jnp.bfloat16)
        xa, xc, xd = xh[a, a], xh[b, a], xh[b, b]
        na = x_ref[a, a] - nn(faa, xa)
        nc = x_ref[b, a] - (nn(fca, xa) + nn(fdd, xc))
        nd = x_ref[b, b] - nn(fdd, xd)
        x_ref[a, a] = na
        x_ref[b, a] = nc
        x_ref[b, b] = nd
        if not fine:
            xh[a, a] = na.astype(jnp.bfloat16)
            xh[b, a] = nc.astype(jnp.bfloat16)
            xh[b, b] = nd.astype(jnp.bfloat16)

    def step(_, carry):
        eaa, eca, edd = residual((xh,), (sh,), None)
        update((minus_eye(eaa), eca, minus_eye(edd)), False)
        return carry

    lax.fori_loop(0, ROUGH, step, 0)
    hi, lo = split(x_ref[...])
    xh[...] = hi
    xl[...] = lo
    eaa, eca, edd = residual((xh, xl), (sh, sl), None)
    eaa, edd = minus_eye(eaa), minus_eye(edd)
    left = jnp.sum(eaa * eaa) + 2.0 * jnp.sum(eca * eca) + jnp.sum(edd * edd)
    update((eaa, eca, edd), True)
    x_ref[...] = x_ref[...] * dr
    hi, lo = split(x_ref[...])
    xh[...] = hi
    xl[...] = lo
    return left


WIDE = 640


MESH_ID = pl.DeviceIdType.MESH


def place():
    f = lax.axis_index("fsdp")
    return f // 8, (f // 2) % 4, f % 2


def to_device(x, z, core):
    return {"fsdp": (x * 4 + z) * 2 + core}


def greet(peers):
    barrier = pltpu.get_barrier_semaphore()
    for peer in peers:
        pl.semaphore_signal(barrier, inc=1, device_id=peer, device_id_type=MESH_ID)
    pl.semaphore_wait(barrier, len(peers))


def remote(src, dst, sends, recvs, index, peer):
    return pltpu.make_async_remote_copy(
        src_ref=src,
        dst_ref=dst,
        send_sem=sends.at[index],
        recv_sem=recvs.at[index],
        device_id=peer,
        device_id_type=MESH_ID,
    )


def rows_at(start, count):
    return pl.ds(pl.multiple_of(start, count), count)


def start_all(copies):
    for copy in copies:
        copy.start()


def wait_recv_all(copies):
    for copy in copies:
        copy.wait_recv()


def step_body(
    scale, act_in, grads_in, lf_in, rf_in, mom_in, msq_in, lb_in, rb_in, par_in, anc_in, om_in,
    p_own, p_other, mine_out, got_out, first_all,
    msq_out, left_next, right_next, anchor_out, momentum_out, res_out,
    act, grads, lf, rf, mom, msq, lb, rb, par, anc, om,
    g, fac, act2, flip, part, sent_c, got_c, sent_x, got_x, acc_x, sent_z, got_z, sent_f, twice,
    turned, seen, out32, whole, gm, bo, ff, p_ref, pt, q_ref, kept, upd, isl, res_own, res_got,
    s_ref, a21, x_ref, sh, sl, xh, xl, l21h, l21l, sends, recvs, local,
):
    bf, f32 = jnp.bfloat16, jnp.float32
    pairs = (
        (act_in, act), (grads_in, grads), (lf_in, lf), (rf_in, rf), (mom_in, mom), (msq_in, msq),
        (lb_in, lb), (rb_in, rb), (par_in, par), (anc_in, anc), (om_in, om),
    )
    loads = [pltpu.make_async_copy(src, dst, local.at[i]) for i, (src, dst) in enumerate(pairs)]
    start_all(loads)

    def arrive(i):
        loads[i].wait()

    fsdp, island, tensor = lax.axis_index("fsdp"), lax.axis_index("island"), lax.axis_index("tensor")
    x, z, core = place()
    partner = to_device(x, z, 1 - core)
    peers_x = [to_device((x + d) % 4, z, core) for d in (1, 2, 3)]
    peers_z = [to_device(x, (z + d) % 4, core) for d in (1, 2, 3)]
    peers_y = [{"island": (island + d) % 4} for d in (1, 2, 3)]
    other = {"tensor": 1 - tensor}
    chip = (x * 4 + z) * 64
    f, h = slice(0, H), slice(H, N)
    a, b = slice(0, Q4), slice(Q4, H)
    greet([partner, other] + peers_x + peers_z + peers_y)
    started = []

    def launch(copies):
        start_all(copies)
        started.extend(copies)
        return copies

    def tile(i):
        return rows_at(i * Q4, Q4)

    arrive(0)
    swap = launch([remote(act, act2, sends, recvs, 0, other)])

    arrive(2)
    arrive(3)
    near = pl.ds(pl.multiple_of(chip // 128 * 128, 128), WIDE)

    def pack(factor):
        narrow = factor[...].astype(jnp.bfloat16)
        twice[:, :N] = narrow
        twice[:, N:] = narrow
        return twice[:, near]

    @pl.when(core == 0)
    def _():
        fac[rows_at(chip, 32), :] = pack(lf)
        sent_f[...] = pack(rf)

    @pl.when(core == 1)
    def _():
        fac[rows_at(chip + 32, 32), :] = pack(rf)
        sent_f[...] = pack(lf)

    fac_c = launch([remote(sent_f, fac.at[rows_at(chip + core * 32, 32)], sends, recvs, 1, partner)])

    def multiply(o, source):
        flip[...] = source[...].T
        sent_c[o] = nn(flip[rows_at((1 - core) * 256, 256), :], grads[...]).astype(jnp.bfloat16)
        copies = launch([remote(sent_c.at[o], got_c.at[o], sends, recvs, 2 + o, partner)])
        part[o] = nn(flip[rows_at(core * 256, 256), :], grads[...])
        return copies

    def reduce_x(o, copies):
        wait_recv_all(copies)
        part[o] += got_c[o].astype(jnp.float32)
        for d in (1, 2, 3):
            sent_x[o, d - 1] = part[o, rows_at((x + d) % 4 * 64, 64), :].astype(jnp.bfloat16)
        return launch([
            remote(sent_x.at[o, d], got_x.at[o, d], sends, recvs, 4 + o * 3 + d, peers_x[d]) for d in range(3)
        ])

    def reduce_z(o, copies):
        wait_recv_all(copies)
        total = part[o, rows_at(x * 64, 64), :]
        for d in range(3):
            total += got_x[o, d].astype(jnp.float32)
        acc_x[o] = total
        for d in (1, 2, 3):
            sent_z[o, d - 1] = acc_x[o, rows_at((z + d) % 4 * 16, 16), :].astype(jnp.bfloat16)
        return launch([
            remote(sent_z.at[o, d], got_z.at[o, d], sends, recvs, 10 + o * 3 + d, peers_z[d]) for d in range(3)
        ])

    def base(o):
        half = tensor if o == 0 else 1 - tensor
        return half * 512 + core * 256

    def gather_z(o, copies):
        wait_recv_all(copies)
        total = acc_x[o, rows_at(z * 16, 16), :]
        for d in range(3):
            total += got_z[o, d].astype(jnp.float32)
        mine = rows_at(base(o) + x * 64 + z * 16, 16)
        g[mine, :] = (total * scale).astype(jnp.bfloat16)
        return launch([remote(g.at[mine], g.at[mine], sends, recvs, 16 + o * 3 + d, peers_z[d]) for d in range(3)])

    def gather_x(o, copies):
        wait_recv_all(copies)
        mine = rows_at(base(o) + x * 64, 64)
        return launch([remote(g.at[mine], g.at[mine], sends, recvs, 22 + o * 3 + d, peers_x[d]) for d in range(3)])

    def gather_c(o, copies):
        wait_recv_all(copies)
        mine = rows_at(base(o), 256)
        return launch([remote(g.at[mine], g.at[mine], sends, recvs, 28 + o, partner)])

    arrive(1)
    c0 = multiply(0, act)
    x0 = reduce_x(0, c0)
    z0 = reduce_z(0, x0)
    wait_recv_all(swap)
    c1 = multiply(1, act2)
    wait_recv_all(fac_c)
    mine_z = rows_at(chip, 64)
    fac_z = launch([remote(fac.at[mine_z], fac.at[mine_z], sends, recvs, 30 + d, peers_z[d]) for d in range(3)])
    gz0 = gather_z(0, z0)
    x1 = reduce_x(1, c1)
    gx0 = gather_x(0, gz0)
    z1 = reduce_z(1, x1)
    gz1 = gather_z(1, z1)
    gx1 = gather_x(1, gz1)
    wait_recv_all(fac_z)
    mine_x = rows_at(x * 256, 256)
    fac_x = launch([remote(fac.at[mine_x], fac.at[mine_x], sends, recvs, 33 + d, peers_x[d]) for d in range(3)])
    arrive(6)
    arrive(7)
    turned[...] = lb[:, pl.ds(pl.multiple_of(fsdp // 4 * 128, 128), 128)].T

    @pl.when(core == 0)
    def _():
        bo[...] = lb[...]

    @pl.when(core == 1)
    def _():
        bo[...] = rb[...]

    gc0 = gather_c(0, gx0)
    gc1 = gather_c(1, gx1)
    wait_recv_all(gc0)
    wait_recv_all(gc1)

    half = nn(turned[rows_at(fsdp % 4 * 32, 32), :], g[...]).astype(bf)
    rotated = nn(half, rb[...])
    arrive(4)
    arrive(5)
    first = BETA_ONE * mom[...] + (1.0 - BETA_ONE) * rotated
    second = BETA_TWO * msq[...] + (1.0 - BETA_TWO) * rotated * rotated
    msq_out[...] = second
    normed = (first / (jnp.sqrt(second) + ADAM_EPS)).astype(bf)
    first = first.astype(bf)

    @pl.when(core == 0)
    def _():
        seen[rows_at(chip, 32), :] = normed
        out32[...] = first
        gm[...] = g[...]

    @pl.when(core == 1)
    def _():
        seen[rows_at(chip + 32, 32), :] = first
        out32[...] = normed
        gm[...] = g[...].T

    seen_c = launch([remote(out32, seen.at[rows_at(chip + core * 32, 32)], sends, recvs, 40, partner)])

    def square_rows(i, c):
        ff[tile(i), :] = nt(gm[tile(i), :], gm[...]) * ((1.0 - FACTOR_BETA) / N)
        return c

    lax.fori_loop(0, 4, square_rows, 0)
    wait_recv_all(seen_c)
    mine = rows_at(chip, 64)
    seen_z = launch([remote(seen.at[mine], seen.at[mine], sends, recvs, 41 + d, peers_z[d]) for d in range(3)])
    away = rows_at(chip + (1 - core) * 32, 32)
    kept_c = launch([remote(ff.at[away], kept, sends, recvs, 45, partner)])

    wait_recv_all(fac_x)
    for i in range(8):
        for k in range(5):
            j = (i + k) % 8
            block = fac[i * 128:(i + 1) * 128, k * 128:(k + 1) * 128]
            whole[i * 128:(i + 1) * 128, j * 128:(j + 1) * 128] = block
            if 0 < k < 4:
                whole[j * 128:(j + 1) * 128, i * 128:(i + 1) * 128] = block.T

    def power_rows(i, c):
        nxt = (FACTOR_BETA * whole[tile(i), :].astype(f32) + ff[tile(i), :]).astype(bf)
        p_ref[tile(i), :] = nn(nxt, bo[...]).astype(bf)
        return c

    lax.fori_loop(0, 4, power_rows, 0)
    p_copy = pltpu.make_async_copy(p_ref, p_own, local.at[11])
    p_copy.start()
    p_swap = launch([remote(p_ref, p_other, sends, recvs, 44, partner)])

    pt[...] = p_ref[...].T
    s_ref[...] = nt(pt[f, :], pt[f, :])
    a21[...] = nt(pt[h, :], pt[f, :])
    r1 = leaf(s_ref, x_ref, sh, sl, xh, xl)

    wait_recv_all(seen_z)
    mine = rows_at(x * 256, 256)
    seen_x = launch([remote(seen.at[mine], seen.at[mine], sends, recvs, 46 + d, peers_x[d]) for d in range(3)])

    def by_x(t):
        ta = tuple(v[:, a] for v in t)
        xa, x2 = (xh[a, a], xl[a, a]), (xh[b, :], xl[b, :])
        if len(t) == 1:
            return nt(ta[0], xa[0]) + nt(ta[0], xa[1]), nt(t[0], x2[0]) + nt(t[0], x2[1])
        return nt3(ta, xa), nt3(t, x2)

    def l_rows(i, c):
        u, v = by_x(split(a21[tile(i), :]))
        l21h[tile(i), a], l21l[tile(i), a] = split(u)
        l21h[tile(i), b], l21l[tile(i), b] = split(v)
        return c

    lax.fori_loop(0, 2, l_rows, 0)
    s_ref[...] = nt(pt[h, :], pt[h, :]) - nt3((l21h[...], l21l[...]), (l21h[...], l21l[...]))

    def q1_rows(i, c):
        u, v = by_x((p_ref[tile(i), f],))
        q_ref[tile(i), a], pt[tile(i), a] = split(u)
        q_ref[tile(i), b], pt[tile(i), b] = split(v)
        return c

    lax.fori_loop(0, 4, q1_rows, 0)
    first_half, last_half = pl.ds(0, H), pl.ds(H, H)
    q1_copy = pltpu.make_async_copy(q_ref.at[:, first_half], mine_out.at[:, first_half], local.at[13])
    q1_copy.start()
    q1_swap = launch([remote(q_ref.at[:, first_half], got_out.at[:, first_half], sends, recvs, 49, partner)])

    wait_recv_all(kept_c)
    ours, theirs = ff[rows_at(chip + core * 32, 32), :], kept[...]
    left_next[...] = FACTOR_BETA * lf[...] + jnp.where(core == 0, ours, theirs)
    right_next[...] = FACTOR_BETA * rf[...] + jnp.where(core == 0, theirs, ours)

    r2 = leaf(s_ref, x_ref, sh, sl, xh, xl)
    res_own[...] = jnp.full((8, 128), jnp.maximum(r1, r2), f32)
    res_c = launch([remote(res_own, res_got, sends, recvs, 50, partner)])

    wait_recv_all(seen_x)
    upd_c = remote(upd.at[pl.ds(32, 32)], upd.at[pl.ds(32, 32)], sends, recvs, 51, partner)
    first_copy = pltpu.make_async_copy(seen, first_all, local.at[12])
    first_c = remote(seen, first_all, sends, recvs, 52, partner)

    @pl.when(core == 0)
    def _():
        back = nn(lb[rows_at(chip, 64), :], seen[...]).astype(bf)
        upd[...] = nt(back, rb[...])
        upd_c.start()

    @pl.when(core == 1)
    def _():
        first_copy.start()
        first_c.start()

    def q2_rows(i, c):
        t = p_ref[tile(i), h].astype(f32) - nt3((q_ref[tile(i), f], pt[tile(i), f]), (l21h[...], l21l[...]))
        u, v = by_x(split(t))
        q_ref[tile(i), H:H + Q4] = u.astype(bf)
        q_ref[tile(i), H + Q4:N] = v.astype(bf)
        return c

    lax.fori_loop(0, 4, q2_rows, 0)
    q2_copy = pltpu.make_async_copy(q_ref.at[:, last_half], mine_out.at[:, last_half], local.at[14])
    q2_copy.start()
    q2_swap = launch([remote(q_ref.at[:, last_half], got_out.at[:, last_half], sends, recvs, 53, partner)])

    @pl.when(core == 1)
    def _():
        upd_c.wait_recv()

    arrive(8)
    arrive(9)
    delta = anc[...] - (par[...] - INNER_RATE * upd[rows_at(core * 32, 32), :])
    isl[island] = delta
    isl_y = launch([remote(isl.at[island], isl.at[island], sends, recvs, 54 + d, peers_y[d]) for d in range(3)])


    wait_recv_all(isl_y)
    average = (isl[0] + isl[1] + isl[2] + isl[3]) / 4.0
    arrive(10)
    momentum = OUTER_MOMENT * om[...] + average
    momentum_out[...] = momentum
    anchor_out[...] = anc[...] - OUTER_RATE * (average + OUTER_MOMENT * momentum)
    wait_recv_all(res_c)
    res_out[...] = jnp.maximum(res_own[...], res_got[...])
    wait_recv_all(p_swap)
    wait_recv_all(q1_swap)
    wait_recv_all(q2_swap)
    p_copy.wait()
    q1_copy.wait()
    q2_copy.wait()

    @pl.when(core == 0)
    def _():
        first_c.wait_recv()
        upd_c.wait_send()

    @pl.when(core == 1)
    def _():
        first_copy.wait()
        first_c.wait_send()

    for copy in started:
        copy.wait_send()


def step(scale, operands):
    bf, f32 = jnp.bfloat16, jnp.float32
    vm, hbm = pl.BlockSpec(memory_space=pltpu.VMEM), pl.BlockSpec(memory_space=pl.ANY)
    square = jax.ShapeDtypeStruct((N, N), bf)
    strip = jax.ShapeDtypeStruct((32, N), f32)
    big = pltpu.VMEM((N, N), bf)
    thin = pltpu.VMEM((32, N), f32)
    return pl.pallas_call(
        functools.partial(step_body, scale),
        out_shape=(square,) * 5 + (strip,) * 5 + (jax.ShapeDtypeStruct((8, 128), f32),),
        in_specs=[hbm] * 11,
        out_specs=(hbm,) * 5 + (vm,) * 6,
        scratch_shapes=[
            pltpu.VMEM((512, 512), bf), pltpu.VMEM((512, N), bf), thin, thin, thin, thin, big, big, thin, thin, thin,
            big,
            pltpu.VMEM((N, WIDE), bf),
            pltpu.VMEM((512, 512), bf),
            pltpu.VMEM((512, 512), bf),
            pltpu.VMEM((2, 256, N), f32),
            pltpu.VMEM((2, 256, N), bf),
            pltpu.VMEM((2, 256, N), bf),
            pltpu.VMEM((2, 3, 64, N), bf),
            pltpu.VMEM((2, 3, 64, N), bf),
            pltpu.VMEM((2, 64, N), f32),
            pltpu.VMEM((2, 3, 16, N), bf),
            pltpu.VMEM((2, 3, 16, N), bf),
            pltpu.VMEM((32, WIDE), bf),
            pltpu.VMEM((32, 2 * N), bf),
            pltpu.VMEM((128, N), bf),
            big,
            pltpu.VMEM((32, N), bf),
            big, big, big,
            pltpu.VMEM((N, N), f32),
            big, big, big,
            thin,
            pltpu.VMEM((64, N), f32),
            pltpu.VMEM((4, 32, N), f32),
            pltpu.VMEM((8, 128), f32),
            pltpu.VMEM((8, 128), f32),
            pltpu.VMEM((H, H), f32), pltpu.VMEM((H, H), f32), pltpu.VMEM((H, H), f32),
        ] + [pltpu.VMEM((H, H), bf)] * 6 + [
            pltpu.SemaphoreType.DMA((57,)),
            pltpu.SemaphoreType.DMA((57,)),
            pltpu.SemaphoreType.DMA((15,)),
        ],
        compiler_params=pltpu.CompilerParams(
            collective_id=0, has_side_effects=True, vmem_limit_bytes=VMEM_LIMIT
        ),
        name="step",
    )(*operands)


def orth_columns(power, gram, work, flip, out):
    flip[...] = power[...].T

    def fill(i, c):
        rows = rows_at(i * 128, 128)
        gram[rows, :] = nt(flip[rows, :], flip[...])
        work[rows, :] = power[rows, :].astype(jnp.float32)
        return c

    lax.fori_loop(0, 8, fill, 0)
    lane = lax.broadcasted_iota(jnp.int32, (1, N), 1)

    def column(k, c):
        row = gram[pl.ds(k, 1), :]
        at = lane == k
        scale = 1.0 / jnp.sqrt(jnp.sum(jnp.where(at, row, 0.0), 1, keepdims=True))
        upper = jnp.where(lane >= k, row * scale, 0.0)
        after = jnp.where(at, 0.0, upper)

        def strip(i, c):
            rows = rows_at(i * 128, 128)
            old = gram[rows, :]
            gram[rows, :] = old - jnp.sum(jnp.where(at, old, 0.0), 1, keepdims=True) * scale * upper
            old = work[rows, :]
            done = jnp.sum(jnp.where(at, old, 0.0), 1, keepdims=True) * scale
            work[rows, :] = jnp.where(at, done, old - done * after)
            return c

        return lax.fori_loop(0, 8, strip, c)

    lax.fori_loop(0, N, column, 0)
    out[...] = work[...].astype(jnp.bfloat16)


def finish_body(
    p_own, p_other, mine, got, first_in, lb_in, rb_in, msq, left_next, right_next, anchor, momentum, res_in,
    anchor_out, momentum_out, moment_out, msq_out, lnext_out, rnext_out, left_out, right_out,
    lb, rb, first, left_v, right_v, rows, res, turned, mrows, gram, work, power, flip, local,
):
    fsdp = lax.axis_index("fsdp")
    core = fsdp % 2
    load_res, load_l, load_f, load_r = [
        pltpu.make_async_copy(src, dst, local.at[i])
        for i, (src, dst) in enumerate(((res_in, res), (lb_in, lb), (first_in, first), (rb_in, rb)))
    ]
    start_all([load_res, load_l])

    def twice(v, mm, m):
        both = mm(jnp.concatenate(split(v), 0), m[...])
        return both[:32] + both[32:]

    passed = [
        (
            pltpu.make_async_copy(src, rows.at[i], local.at[6 + i]),
            pltpu.make_async_copy(rows.at[i], dst, local.at[6 + i]),
        )
        for i, (src, dst) in enumerate((
            (anchor, anchor_out), (momentum, momentum_out), (msq, msq_out), (left_next, lnext_out), (right_next, rnext_out),
        ))
    ]
    for copy_in, _ in passed:
        copy_in.start()

    def close(left, right):
        outs = [
            pltpu.make_async_copy(left, left_out, local.at[11]),
            pltpu.make_async_copy(right, right_out, local.at[12]),
        ]
        start_all(outs)
        columns = pl.ds(pl.multiple_of(fsdp // 4 * 128, 128), 128)
        turned[...] = left[:, columns].T
        turn = nn(turned[rows_at(fsdp % 4 * 32, 32), :], lb[...])
        load_f.wait()
        part = twice(turn, nn, first)
        load_r.wait()
        part = twice(part, nt, rb)
        mrows[...] = twice(part, nn, right)
        last = pltpu.make_async_copy(mrows, moment_out, local.at[13])
        last.start()
        for copy_in, copy_out in passed:
            copy_in.wait()
            copy_out.start()
        for _, copy_out in passed:
            copy_out.wait()
        for copy in outs + [last]:
            copy.wait()

    def fetch(left, right):
        load_left = pltpu.make_async_copy(left, left_v, local.at[4])
        load_right = pltpu.make_async_copy(right, right_v, local.at[5])
        start_all([load_left, load_f, load_r, load_right])
        load_l.wait()
        load_left.wait()
        load_right.wait()

    load_res.wait()
    good = jnp.sum(res[...]) < RESIDUAL_LIMIT * 1024.0

    @pl.when(jnp.logical_and(good, core == 0))
    def _():
        fetch(mine, got)

    @pl.when(jnp.logical_and(good, core == 1))
    def _():
        fetch(got, mine)

    @pl.when(jnp.logical_not(good))
    def _():
        def redo(side, out):
            @pl.when(core == side)
            def _():
                pltpu.sync_copy(p_own, power)

            @pl.when(core != side)
            def _():
                pltpu.sync_copy(p_other, power)

            orth_columns(power, gram, work, flip, out)

        start_all([load_f, load_r])
        load_l.wait()
        redo(0, left_v)
        redo(1, right_v)

    close(left_v, right_v)


def finish(operands):
    bf, f32 = jnp.bfloat16, jnp.float32
    hbm = pl.BlockSpec(memory_space=pl.ANY)
    square = jax.ShapeDtypeStruct((N, N), bf)
    strip = jax.ShapeDtypeStruct((32, N), f32)
    big = pltpu.VMEM((N, N), bf)
    return pl.pallas_call(
        finish_body,
        out_shape=(strip,) * 6 + (square,) * 2,
        in_specs=[hbm] * 13,
        out_specs=(hbm,) * 8,
        scratch_shapes=[
            big, big, big, big, big, pltpu.VMEM((5, 32, N), f32), pltpu.VMEM((8, 128), f32),
            pltpu.VMEM((128, N), bf), pltpu.VMEM((32, N), f32),
            pltpu.VMEM((N, N), f32), pltpu.VMEM((N, N), f32), big, big,
            pltpu.SemaphoreType.DMA((14,)),
        ],
        compiler_params=pltpu.CompilerParams(vmem_limit_bytes=FINISH_LIMIT),
        name="finish",
    )(*operands)


def per_device(
    activations,
    out_grads,
    moment,
    moment_sq,
    left_factor,
    right_factor,
    left_basis,
    right_basis,
    params,
    anchor,
    outer_momentum,
):
    scale = 1.0 / math.sqrt(activations.shape[1] * lax.axis_size("fsdp"))
    left_old, right_old = left_basis[0, 0], right_basis[0, 0]
    operands = (
        activations[0], out_grads[0], left_factor[0, 0], right_factor[0, 0], moment[0, 0], moment_sq[0, 0],
        left_old, right_old, params[0, 0], anchor[0], outer_momentum[0],
    )
    power, power_other, mine, got, first_all, *rows, residual = step(scale, operands)
    anchor_next, momentum_next, moment_next, second_moment, left_next, right_next, left_new, right_new = finish(
        (power, power_other, mine, got, first_all, left_old, right_old, *rows, residual)
    )
    return (
        anchor_next[None],
        momentum_next[None],
        moment_next[None, None],
        second_moment[None, None],
        left_next[None, None],
        right_next[None, None],
        left_new[None, None],
        right_new[None, None],
    )


def solution(mesh):
    in_specs = (
        P("island", "fsdp", "tensor"),
        P("island", "fsdp", "tensor"),
        P("island", "tensor", "fsdp", None),
        P("island", "tensor", "fsdp", None),
        P("island", "tensor", "fsdp", None),
        P("island", "tensor", "fsdp", None),
        P("island", "tensor", None, None),
        P("island", "tensor", None, None),
        P("island", "tensor", "fsdp", None),
        P("tensor", "fsdp", None),
        P("tensor", "fsdp", None),
    )
    out_specs = (
        P("tensor", "fsdp", None),
        P("tensor", "fsdp", None),
        P("island", "tensor", "fsdp", None),
        P("island", "tensor", "fsdp", None),
        P("island", "tensor", "fsdp", None),
        P("island", "tensor", "fsdp", None),
        P("island", "tensor", None, None),
        P("island", "tensor", None, None),
    )
    return jax.shard_map(
        per_device, mesh=mesh, in_specs=in_specs, out_specs=out_specs, check_vma=False
    )
```
